256 devices in a mesh: ctx: 32 (over x, z), head: 8 (over y, core).
Axes of the slice: x: 4, y: 4, z: 8, core: 2. Of those that a mesh axis runs over, the one named last changes fastest.
Arguments:
- channels_in: bfloat16 [49152, 8192], P('ctx', 'head'), may hold values from -6 to 6
- state_maps: bfloat16 [49152, 2, 1024], P('ctx', None, 'head'), may hold values from -6 to 6
- gate_in: bfloat16 [49152, 8192], P('ctx', 'head'), may hold values from -6 to 6
- step_raw: float32 [49152, 128], P('ctx', 'head'), may hold values from -1.2 to 80
- convolution_channel_taps: float32 [4, 8192], P(None, 'head'), may hold values from -3 to 3
- conv_maps: float32 [4, 2, 1024], P(None, None, 'head'), may hold values from -3 to 3
- head_rates: float32 [2, 128], P(None, 'head'), may hold values from -8 to 0
- skip_gain: float32 [128], P('head'), may hold values from 0.5 to 2
- norm_gain: float32 [8192], P('head'), may hold values from 0.5 to 1.5
Outputs:
- relaid: bfloat16 [49152, 8192], P(('ctx', 'head'))
The draws below stay inside these ranges and needn't reach their ends.
All inputs are finite; a program needn't handle non-finite values.
Results may differ from the reference program's by a relative error of at most 0.006.
Values may be sent and summed in bfloat16 or wider, within the bound.
A program may use at most 128 MiB of HBM per device.

```python
import jax
import jax.numpy as jnp
from jax import lax

HEADS = 128
HEAD_DIM = 64
STATE = 128
GROUPS = 8
TAPS = 4
STRETCH = 256
LARGE_STEP_COUNT = 6
D_INNER = 8192
SEQUENCE_LENGTH = 49152


def large_step_rows(key):
    return jax.random.randint(jax.random.fold_in(key, 4711), (LARGE_STEP_COUNT,), 0, SEQUENCE_LENGTH)


def draw_channels_in(key, part):
    noise_key = jax.random.fold_in(key, 11)
    noise = jnp.clip(jax.random.normal(noise_key, (SEQUENCE_LENGTH, D_INNER), jnp.float32), -6.0, 6.0)
    sequence_positions = jnp.arange(SEQUENCE_LENGTH, dtype=jnp.int32)[:, None]
    position_distance = sequence_positions - large_step_rows(key)[None, :]
    nearby = jnp.any((position_distance >= 0) & (position_distance < TAPS), axis=1)
    factor = jnp.where(nearby, 0.02, 1.0)
    return (noise * factor[:, None]).astype(jnp.bfloat16)


def draw_step_raw(key, part):
    noise = jax.random.uniform(jax.random.fold_in(key, 21), (SEQUENCE_LENGTH, HEADS), jnp.float32, -0.7, 0.7)
    blocks = jax.random.uniform(jax.random.fold_in(key, 22), (SEQUENCE_LENGTH // STRETCH, 1, HEADS), jnp.float32, -0.5, 0.5)
    shifted = (noise.reshape(SEQUENCE_LENGTH // STRETCH, STRETCH, HEADS) + blocks).reshape(SEQUENCE_LENGTH, HEADS)
    large_step_mask = jnp.any(jnp.arange(SEQUENCE_LENGTH, dtype=jnp.int32)[:, None] == large_step_rows(key)[None, :], axis=1)
    return jnp.where(large_step_mask[:, None], 80.0, shifted).astype(jnp.float32)


def draw_head_rates(key, part):
    ranking = jax.random.permutation(jax.random.fold_in(key, 31), HEADS)
    quick_share = HEADS // 2
    quick = ranking < quick_share
    spread = jax.random.uniform(jax.random.fold_in(key, 32), (2, HEADS), jnp.float32)
    half_log = 0.5 * jnp.log(jnp.float32(SEQUENCE_LENGTH))
    slow_bias = -half_log - 0.3 + 0.6 * spread[0]
    quick_bias = -1.8 + 0.6 * spread[0]
    slow_rate = -half_log + jnp.log(0.5) + jnp.log(3.0) * spread[1]
    quick_rate = jnp.log(0.1) + jnp.log(1.667) * spread[1]
    return jnp.stack([jnp.where(quick, quick_bias, slow_bias), jnp.where(quick, quick_rate, slow_rate)]).astype(jnp.float32)


def block_scale(own_key, extent, shards, smallest, high):
    factor_of, own = 1.0, jax.random.fold_in(own_key, 6)
    for dim, parts in shards:
        heights = jnp.exp(jax.random.uniform(jax.random.fold_in(own, dim), (parts,), jnp.float32, smallest / len(shards), high / len(shards)))
        factor_of = factor_of * jnp.repeat(heights, extent[dim] // parts).reshape([-1 if axis == dim else 1 for axis in range(len(extent))])
    return factor_of


def normal_values(stream_key, dims, scale, reach, shards=(), held_as=jnp.bfloat16):
    values = scale * jax.random.normal(stream_key, dims, jnp.float32)
    if shards:
        values = values * block_scale(stream_key, dims, shards, -0.22, 0.18)
    return jnp.clip(values, -reach, reach).astype(held_as)


def setup_inputs(seed: int = 0) -> dict:
    seeds = jax.random.split(jax.random.key(seed), 10)
    return {
        "channels_in": draw_channels_in(jax.random.fold_in(seeds[9], 71), 0),
        "state_maps": normal_values(seeds[1], (SEQUENCE_LENGTH, 2, GROUPS * STATE), 1.0, 6.0, ((0, 32), (2, 8))),
        "gate_in": normal_values(seeds[2], (SEQUENCE_LENGTH, D_INNER), 1.0, 6.0, ((0, 32), (1, 8))),
        "step_raw": draw_step_raw(jax.random.fold_in(seeds[9], 71), 0),
        "convolution_channel_taps": normal_values(seeds[4], (TAPS, D_INNER), TAPS ** -0.5, 3.0, ((1, 8),), jnp.float32),
        "conv_maps": normal_values(seeds[5], (TAPS, 2, GROUPS * STATE), TAPS ** -0.5, 3.0, ((2, 8),), jnp.float32),
        "head_rates": draw_head_rates(jax.random.fold_in(seeds[9], 71), 0),
        "skip_gain": jnp.clip(0.5 + 1.5 * jax.random.uniform(seeds[7], (HEADS,), jnp.float32) ** block_scale(seeds[7], (HEADS,), ((0, 8),), -0.2, 0.2), 0.5, 2.0),
        "norm_gain": jnp.clip(1.0 + 0.1 * jax.random.normal(seeds[8], (D_INNER,), jnp.float32), 0.5, 1.5),
    }


HIGHEST_PRECISION = lax.Precision.HIGHEST
EPSILON = 1e-05

def conv_silu(sequence, kernel):
    padded = jnp.concatenate([jnp.zeros((TAPS - 1,) + sequence.shape[1:], jnp.float32), sequence.astype(jnp.float32)], 0)
    summed = jnp.zeros(sequence.shape, jnp.float32)
    for offset in range(TAPS):
        summed = summed + kernel[offset] * padded[offset:offset + SEQUENCE_LENGTH]
    return jax.nn.silu(summed).astype(jnp.bfloat16)

def stretch_terms(pieces):
    values, b_maps, c_maps, step_sizes, log_rates = pieces
    length = values.shape[0]
    cumlog = jnp.cumsum(log_rates, axis=0)
    causal = jnp.arange(length)[:, None] >= jnp.arange(length)[None, :]
    log_gaps = cumlog[:, None] - cumlog[None, :]
    decays = jnp.exp(jnp.where(causal[:, :, None, None], log_gaps, -jnp.inf))
    scores = jnp.einsum('tgn,sgn->tsg', c_maps, b_maps, preferred_element_type=jnp.float32)
    weights = (scores[..., None] * decays * step_sizes[None]).astype(jnp.bfloat16)
    values_wide = values.astype(jnp.float32)
    inside = jnp.einsum('tsgh,sghp->tghp', weights.astype(jnp.float32), values_wide, precision=HIGHEST_PRECISION)
    tail_weights = jnp.exp(cumlog[-1][None] - cumlog) * step_sizes
    tail = (tail_weights[..., None] * values_wide).astype(jnp.bfloat16)
    b_wide = b_maps.astype(jnp.float32)
    summary = jnp.einsum('sghp,sgn->ghpn', tail.astype(jnp.float32), b_wide, precision=HIGHEST_PRECISION)
    return (inside, summary, cumlog)

def reference(channels_in, state_maps, gate_in, step_raw, convolution_channel_taps, conv_maps, head_rates, skip_gain, norm_gain):
    conv_x = conv_silu(channels_in, convolution_channel_taps)
    conv_bc = conv_silu(state_maps, conv_maps)
    step_sizes = jax.nn.softplus(step_raw + head_rates[0][None, :])
    log_rates = -jnp.exp(head_rates[1])[None, :] * step_sizes
    stretch_count = SEQUENCE_LENGTH // STRETCH
    per_group = HEADS // GROUPS
    values = conv_x.reshape(stretch_count, STRETCH, GROUPS, per_group, HEAD_DIM)
    b_maps = conv_bc[:, 0].reshape(stretch_count, STRETCH, GROUPS, STATE)
    c_maps = conv_bc[:, 1].reshape(stretch_count, STRETCH, GROUPS, STATE)
    step_sizes = step_sizes.reshape(stretch_count, STRETCH, GROUPS, per_group)
    log_rates = log_rates.reshape(stretch_count, STRETCH, GROUPS, per_group)

    def advance(carried, pieces):
        inside, summary, cumlog = stretch_terms(pieces)
        c_block = pieces[2].astype(jnp.float32)
        from_state = jnp.einsum('tgn,ghpn->tghp', c_block, carried, precision=HIGHEST_PRECISION) * jnp.exp(cumlog)[..., None]
        renewed = jnp.exp(cumlog[-1])[..., None, None] * carried + summary
        return (renewed, inside + from_state)
    initial = jnp.zeros((GROUPS, per_group, HEAD_DIM, STATE), jnp.float32)
    final_state, outputs = lax.scan(advance, initial, (values, b_maps, c_maps, step_sizes, log_rates))
    skipped = skip_gain.reshape(GROUPS, per_group)[..., None] * values.astype(jnp.float32)
    ssm_out = (outputs + skipped).reshape(SEQUENCE_LENGTH, GROUPS, per_group * HEAD_DIM)
    gating = jax.nn.silu(gate_in.astype(jnp.float32)).reshape(SEQUENCE_LENGTH, GROUPS, per_group * HEAD_DIM)
    gated_out = ssm_out * gating
    inverse_rms = lax.rsqrt(lax.optimization_barrier(jnp.mean(gated_out * gated_out, axis=-1, keepdims=True)) + EPSILON)
    normed = gated_out * inverse_rms * norm_gain.reshape(GROUPS, per_group * HEAD_DIM)
    return normed.reshape(SEQUENCE_LENGTH, HEADS * HEAD_DIM).astype(jnp.bfloat16)
```

```python
import jax
import jax.numpy as jnp
from jax import lax
from jax.experimental import pallas as pl
from jax.experimental.pallas import tpu as pltpu
from jax.sharding import PartitionSpec as P

HEAD_DIM = 64
STATE = 128
TAPS = 4
EPSILON = 1e-05
HI = lax.Precision.HIGHEST
MESH = pl.DeviceIdType.MESH
F32 = jnp.float32
BF16 = jnp.bfloat16

ROWS = 1536
COLS = 1024
HEADS = 16
BLOCK = 128
BLOCKS = ROWS // BLOCK
PARTS = 4
WIDE = COLS // PARTS
ZS = 8
XS = 4
SLICE = STATE // ZS
LEAD = 16
SUB = 64


def iota(shape, dim):
    return lax.broadcasted_iota(jnp.int32, shape, dim)


def dot(a, b, precision=None):
    return jnp.dot(a, b, precision=precision, preferred_element_type=F32)


def silu(v):
    half = 0.5 * v
    return half + half * jnp.tanh(half)


def split_in_two(v):
    high = v.astype(BF16)
    return high, (v - high.astype(F32)).astype(BF16)


def kernel(
    ch_hbm, bc_hbm, gate_hbm, step_hbm, taps, map_taps, rates, skip, gain, out,
    ch, bc, gate, step, wide, xs, bs, bt, cs, cum_v, step_v, tails, decays, spread,
    rows_v, skip_v, state, entering, y0, staged, gated_v,
    zs, z1, prefix, xt, x1, back, incoming, dl, dl_in, tl, tl_in, za, xa,
    in_sem, halo_s, halo_r, dl_s, dl_r, tl_s, tl_r, z1_s, z1_r, x1_s, x1_r, z2_s, z2_r,
    y_s, y_r, own_sem,
):
    c = lax.axis_index("ctx")
    me = lax.axis_index("head")
    x, z = c // ZS, c % ZS
    y, core = me // 2, me % 2

    loads = [pltpu.make_async_copy(step_hbm, step, in_sem.at[0])]
    loads.append(pltpu.make_async_copy(bc_hbm, bc.at[pl.ds(LEAD, ROWS)], in_sem.at[1]))
    for q in range(PARTS):
        part = pl.ds(q * WIDE, WIDE)
        loads.append(
            pltpu.make_async_copy(
                ch_hbm.at[:, part], ch.at[pl.ds(LEAD, ROWS), part], in_sem.at[2 + q]
            )
        )
    loads.append(pltpu.make_async_copy(gate_hbm, gate, in_sem.at[2 + PARTS]))
    for load in loads:
        load.start()

    def z_peer(d):
        return (x * ZS + (z + d) % ZS, me)

    def x_peer(d):
        return (((x + d) % XS) * ZS + z, me)

    after, before = ((c + 1) % (XS * ZS), me), ((c + XS * ZS - 1) % (XS * ZS), me)
    peers = [z_peer(d) for d in range(1, ZS)] + [x_peer(d) for d in range(1, XS)]
    peers += [(c, (me + d) % 8) for d in range(1, 8)] + [after, before]
    barrier = pltpu.get_barrier_semaphore()
    for peer in peers:
        pl.semaphore_signal(barrier, inc=1, device_id=peer, device_id_type=MESH)

    spread[...] = (iota((2 * HEADS, COLS), 0) % HEADS == iota((2 * HEADS, COLS), 1) // HEAD_DIM).astype(BF16)
    head_of = (iota((HEADS, COLS), 0) == iota((HEADS, COLS), 1) // HEAD_DIM).astype(F32)
    loads[0].wait()
    bias = rates[0:1, :]
    raw = jnp.concatenate(
        [(step[pl.ds(k * BLOCK, BLOCK), :] + bias).T for k in range(BLOCKS)], 0
    )
    rate = jnp.broadcast_to(jnp.exp(rates[1:2, :]), (BLOCK, HEADS)).T
    rate = jnp.concatenate([rate] * BLOCKS, 0)
    sizes = jnp.maximum(raw, 0.0) + jnp.log1p(jnp.exp(-jnp.abs(raw)))
    logs = -rate * sizes
    row, col = iota((BLOCK, BLOCK), 0), iota((BLOCK, BLOCK), 1)
    cum = dot(logs, (row <= col).astype(F32), HI)
    rest = dot(logs, (row > col).astype(F32), HI)
    cum_v[...] = cum
    step_v[...] = sizes
    for source, held in ((jnp.exp(rest) * sizes, tails), (jnp.exp(cum), decays)):
        high, low = split_in_two(source)
        for k in range(BLOCKS):
            held[k, 0:HEADS, :] = high[k * HEADS : (k + 1) * HEADS]
            held[k, HEADS : 2 * HEADS, :] = low[k * HEADS : (k + 1) * HEADS]
    count = BLOCKS * HEADS
    own_head = (iota((count, HEADS), 0) % HEADS == iota((count, HEADS), 1)).astype(F32)
    own_block = (iota((16, count), 0) == iota((16, count), 1) // HEADS).astype(F32)
    totals = dot(own_block, cum[:, BLOCK - 1 : BLOCK] * own_head, HI)
    earlier = dot((iota((16, 16), 0) > iota((16, 16), 1)).astype(F32), totals, HI)
    rows_v[...] = jnp.exp(dot(jnp.concatenate([totals, earlier], 0), head_of, HI))
    skip_v[...] = dot(jnp.broadcast_to(skip[...], (8, HEADS)), head_of, HI)
    whole = jnp.broadcast_to(earlier[BLOCKS : BLOCKS + 1], (8, HEADS))
    dl[...] = dot(whole, (iota((HEADS, 128), 0) == iota((HEADS, 128), 1)).astype(F32), HI)

    pl.semaphore_wait(barrier, len(peers))
    halo = [
        pltpu.make_async_remote_copy(
            src_ref=source.at[pl.ds(ROWS - LEAD, LEAD)], dst_ref=held.at[pl.ds(0, LEAD)],
            send_sem=halo_s.at[i], recv_sem=halo_r.at[i], device_id=after, device_id_type=MESH,
        )
        for i, (source, held) in enumerate(((bc_hbm, bc), (ch_hbm, ch)))
    ]
    for copy in halo:
        copy.start()
    dl_in[z] = dl[...]
    dl_copies = [
        pltpu.make_async_remote_copy(
            src_ref=dl, dst_ref=dl_in.at[z], send_sem=dl_s.at[d], recv_sem=dl_r.at[d],
            device_id=z_peer(d), device_id_type=MESH,
        )
        for d in range(1, ZS)
    ]
    for copy in dl_copies:
        copy.start()

    def conv(held, k, lane, weights):
        start = pl.multiple_of(k * BLOCK, BLOCK)
        block = held[pl.ds(start, BLOCK + LEAD), pl.ds(lane, 128)].astype(F32)
        wide[...] = block
        total = weights[0:1, pl.ds(lane, 128)] * wide[pl.ds(LEAD - 3, BLOCK), :]
        for tap in range(1, TAPS):
            total += weights[tap : tap + 1, pl.ds(lane, 128)] * wide[pl.ds(LEAD - 3 + tap, BLOCK), :]
        return silu(total)

    def maps(k):
        start = pl.multiple_of(k * BLOCK, BLOCK)
        b = conv(bc, k, 0, map_taps)
        bs[pl.ds(start, BLOCK), :] = b.astype(BF16)
        bt[k] = b.T.astype(BF16)
        cs[pl.ds(start, BLOCK), :] = conv(bc, k, STATE, map_taps).astype(BF16)

    loads[1].wait()

    @pl.loop(1, BLOCKS)
    def _(k):
        maps(k)

    for load in loads[2 : 2 + PARTS]:
        load.wait()
    for copy in halo:
        copy.wait()

    @pl.when(c == 0)
    def _():
        bc[pl.ds(0, LEAD), :] = jnp.zeros((LEAD, 2 * STATE), BF16)
        ch[pl.ds(0, LEAD), :] = jnp.zeros((LEAD, COLS), BF16)

    maps(0)

    def local_states(q):
        part = pl.ds(q * WIDE, WIDE)
        state[...] = jnp.zeros((STATE, WIDE), F32)

        @pl.loop(0, BLOCKS)
        def _(k):
            start = pl.multiple_of(k * BLOCK, BLOCK)
            entering[k, :, part] = state[...].astype(BF16)
            weights = lax.dot_general(
                tails[k], spread[:, part], (((0,), (0,)), ((), ())), preferred_element_type=F32
            )
            tail = []
            for i in range(WIDE // 128):
                lane = q * WIDE + i * 128
                value = conv(ch, k, lane, taps).astype(BF16)
                xs[pl.ds(start, BLOCK), pl.ds(lane, 128)] = value
                tail.append((value.astype(F32) * weights[:, i * 128 : (i + 1) * 128]).astype(BF16))
            summary = dot(bt[k], jnp.concatenate(tail, 1))
            state[...] = rows_v[pl.ds(k, 1), part] * state[...] + summary

        zs[q] = state[...].astype(BF16)
        mine = pl.ds(pl.multiple_of(z * SLICE, SLICE), SLICE)
        z1[q, z] = state[mine, :].astype(BF16)
        copies = []
        for d in range(1, ZS):
            there = pl.ds(pl.multiple_of(((z + d) % ZS) * SLICE, SLICE), SLICE)
            copies.append(
                pltpu.make_async_remote_copy(
                    src_ref=zs.at[q, there], dst_ref=z1.at[q, z], send_sem=z1_s.at[q, d],
                    recv_sem=z1_r.at[q, d], device_id=z_peer(d), device_id_type=MESH,
                )
            )
        for copy in copies:
            copy.start()
        return copies

    def shard_decays():
        for copy in dl_copies:
            copy.wait()
        each = jnp.concatenate([dl_in[i, 0:1, :] for i in range(ZS)], 0)
        ahead = dot((iota((ZS, ZS), 0) > iota((ZS, ZS), 1)).astype(F32), each, HI)
        both = jnp.concatenate([each, ahead], 0)
        za[...] = jnp.exp(dot(both[:, :HEADS], head_of, HI))
        tl[...] = jnp.broadcast_to(jnp.sum(each, 0, keepdims=True), (8, 128))
        tl_in[x] = tl[...]
        copies = [
            pltpu.make_async_remote_copy(
                src_ref=tl, dst_ref=tl_in.at[x], send_sem=tl_s.at[d], recv_sem=tl_r.at[d],
                device_id=x_peer(d), device_id_type=MESH,
            )
            for d in range(1, XS)
        ]
        for copy in copies:
            copy.start()
        return copies

    def ring_decays(copies):
        for copy in copies:
            copy.wait()
        each = jnp.concatenate([tl_in[i, 0:1, :] for i in range(XS)] * 2, 0)
        xa[...] = jnp.exp(dot(each[:, :HEADS], head_of, HI))

    def along_z(q, copies):
        part = pl.ds(q * WIDE, WIDE)
        for copy in copies:
            copy.wait()
        total = jnp.zeros((SLICE, WIDE), F32)
        for i in range(ZS):
            prefix[q, i] = total
            total = za[i : i + 1, part] * total + z1[q, i].astype(F32)
        own = total.astype(BF16)
        xt[q] = own
        x1[q, x] = own
        copies = [
            pltpu.make_async_remote_copy(
                src_ref=xt.at[q], dst_ref=x1.at[q, x], send_sem=x1_s.at[q, d],
                recv_sem=x1_r.at[q, d], device_id=x_peer(d), device_id_type=MESH,
            )
            for d in range(1, XS)
        ]
        for copy in copies:
            copy.start()
        return copies

    def along_x(q, copies):
        part = pl.ds(q * WIDE, WIDE)
        for copy in copies:
            copy.wait()
        total = jnp.zeros((SLICE, WIDE), F32)
        for i in range(XS - 1):
            total = jnp.where(i < x, xa[i : i + 1, part] * total + x1[q, i].astype(F32), total)
        for i in range(ZS):
            back[q, i] = (prefix[q, i] + za[ZS + i : ZS + i + 1, part] * total).astype(BF16)
        mine = pl.ds(pl.multiple_of(z * SLICE, SLICE), SLICE)
        incoming[q, mine, :] = back[q, z]
        copies = [
            pltpu.make_async_remote_copy(
                src_ref=back.at[q, (z + d) % ZS], dst_ref=incoming.at[q, mine], send_sem=z2_s.at[q, d],
                recv_sem=z2_r.at[q, d], device_id=z_peer(d), device_id_type=MESH,
            )
            for d in range(1, ZS)
        ]
        for copy in copies:
            copy.start()
        return copies

    def block_at(s):
        r = s % 3
        delta = jnp.where(s < 9, (r * r + r + 1) % 5, 0)
        m = s // 3 - 3 * (s // 9) + (s - 9) * (s // 9)
        there = (y + delta) % 4
        return there, m, 3 * there + m

    def inside(s):
        _, _, k = block_at(s)
        start = pl.multiple_of(k * BLOCK, BLOCK)
        rows = pl.ds(start, BLOCK)
        scores = lax.dot_general(
            cs[rows, :], bs[rows, :], (((1,), (1,)), ((), ())), preferred_element_type=F32
        )
        scores = jnp.where(iota((BLOCK, BLOCK), 0) >= iota((BLOCK, BLOCK), 1), scores, 0.0)
        heads = pl.ds(pl.multiple_of(k * HEADS, HEADS), HEADS)
        across = cum_v[heads, :]
        sizes = step_v[heads, :]
        down = across.T
        left = iota((BLOCK, 128), 1) < HEAD_DIM
        for pair in range(HEADS // 2):
            lanes = pl.ds(pair * 128, 128)
            weights = []
            for h in (2 * pair, 2 * pair + 1):
                gap = jnp.minimum(down[:, h : h + 1] - across[h : h + 1, :], 0.0)
                weights.append((scores * jnp.exp(gap) * sizes[h : h + 1, :]).astype(BF16))
            value = xs[rows, lanes]
            none = jnp.zeros_like(value)
            both = jnp.concatenate([jnp.where(left, value, none), jnp.where(left, none, value)], 0)
            y0[rows, lanes] = dot(jnp.concatenate(weights, 1), both) + skip_v[0:1, lanes] * value.astype(F32)

    def finish(k):
        start = pl.multiple_of(k * BLOCK, BLOCK)
        rows = pl.ds(start, BLOCK)
        squares = jnp.zeros((BLOCK, 128), F32)
        for q in range(PARTS):
            part = pl.ds(q * WIDE, WIDE)
            state_in = entering[k, :, part].astype(F32) + rows_v[pl.ds(16 + k, 1), part] * incoming[q].astype(F32)
            from_state = dot(cs[rows, :], state_in.astype(BF16))
            decay = lax.dot_general(
                decays[k], spread[:, part], (((0,), (0,)), ((), ())), preferred_element_type=F32
            )
            value = (y0[rows, part] + decay * from_state) * silu(gate[rows, part].astype(F32))
            gated_v[:, part] = value
            square = value * value
            squares += square[:, :128] + square[:, 128:]
        scale = lax.rsqrt(jnp.sum(squares, 1, keepdims=True) / COLS + EPSILON)
        for q in range(PARTS):
            part = pl.ds(q * WIDE, WIDE)
            staged[rows, part] = (gated_v[:, part] * scale * gain[0:1, part]).astype(BF16)

    mine = pl.ds(pl.multiple_of(me * COLS, COLS), COLS)

    def send_of(s, i):
        there, m, k = block_at(s)
        j = 2 * m + i
        return pltpu.make_async_remote_copy(
            src_ref=staged.at[pl.ds(pl.multiple_of(k * BLOCK + i * SUB, SUB), SUB)],
            dst_ref=out.at[pl.ds(pl.multiple_of((j % 3) * SUB, SUB), SUB), mine],
            send_sem=y_s.at[2 * s + i], recv_sem=y_r.at[me, j % 3],
            device_id=(c, 2 * there + j // 3), device_id_type=MESH,
        )

    def own_of(s, i):
        _, m, k = block_at(s)
        j = 2 * m + i
        return pltpu.make_async_copy(
            staged.at[pl.ds(pl.multiple_of(k * BLOCK + i * SUB, SUB), SUB)],
            out.at[pl.ds(pl.multiple_of((j % 3) * SUB, SUB), SUB), mine],
            own_sem.at[j % 3],
        )

    def is_own(s, i):
        _, m, _ = block_at(s)
        return (2 * m + i) // 3 == core

    first, second, third = {}, {}, {}
    rings = None
    for q in range(PARTS):
        first[q] = local_states(q)
        if q == 0:
            rings = shard_decays()
        if q >= 1:
            second[q - 1] = along_z(q - 1, first[q - 1])
        if q == 1:
            ring_decays(rings)
        if q >= 2:
            third[q - 2] = along_x(q - 2, second[q - 2])

    def insides(low, high):
        @pl.loop(low, high)
        def _(s):
            inside(s)

    third[PARTS - 2] = along_x(PARTS - 2, second[PARTS - 2])
    insides(0, 4)
    second[PARTS - 1] = along_z(PARTS - 1, first[PARTS - 1])
    insides(4, 8)
    third[PARTS - 1] = along_x(PARTS - 1, second[PARTS - 1])
    insides(8, 12)
    loads[2 + PARTS].wait()
    for q in range(PARTS):
        for copy in third[q]:
            copy.wait()

    @pl.loop(0, 9)
    def _(s):
        _, _, k = block_at(s)
        finish(k)
        for i in range(2):
            send_of(s, i).start()

    @pl.loop(9, 12)
    def _(s):
        _, _, k = block_at(s)
        finish(k)
        for i in range(2):

            @pl.when(is_own(s, i))
            def _():
                own_of(s, i).start()

            @pl.when(jnp.logical_not(is_own(s, i)))
            def _():
                send_of(s, i).start()

    @pl.loop(0, 9)
    def _(s):
        for i in range(2):
            send_of(s, i).wait_send()

    @pl.loop(9, 12)
    def _(s):
        for i in range(2):

            @pl.when(is_own(s, i))
            def _():
                own_of(s, i).wait()

            @pl.when(jnp.logical_not(is_own(s, i)))
            def _():
                send_of(s, i).wait_send()

    @pl.loop(1, 8)
    def _(d):
        source = (me + d) % 8
        lanes = pl.ds(pl.multiple_of(source * COLS, COLS), COLS)
        for j in range(3):
            pltpu.make_async_remote_copy(
                src_ref=staged.at[pl.ds(0, SUB)], dst_ref=out.at[pl.ds(j * SUB, SUB), lanes],
                send_sem=y_s.at[0], recv_sem=y_r.at[source, j],
                device_id=(c, source), device_id_type=MESH,
            ).wait_recv()


def per_device(
    channels_in,
    state_maps,
    gate_in,
    step_raw,
    convolution_channel_taps,
    conv_maps,
    head_rates,
    skip_gain,
    norm_gain,
):
    anywhere = pl.BlockSpec(memory_space=pl.ANY)
    near = pl.BlockSpec(memory_space=pltpu.VMEM)
    dma = pltpu.SemaphoreType.DMA
    return pl.pallas_call(
        kernel,
        out_shape=jax.ShapeDtypeStruct((ROWS // 8, COLS * 8), BF16),
        in_specs=[anywhere] * 4 + [near] * 5,
        out_specs=anywhere,
        scratch_shapes=[
            pltpu.VMEM((LEAD + ROWS, COLS), BF16),
            pltpu.VMEM((LEAD + ROWS, 2 * STATE), BF16),
            pltpu.VMEM((ROWS, COLS), BF16),
            pltpu.VMEM((ROWS, HEADS), F32),
            pltpu.VMEM((LEAD + BLOCK, 128), F32),
            pltpu.VMEM((ROWS, COLS), BF16),
            pltpu.VMEM((ROWS, STATE), BF16),
            pltpu.VMEM((BLOCKS, STATE, BLOCK), BF16),
            pltpu.VMEM((ROWS, STATE), BF16),
            pltpu.VMEM((BLOCKS * HEADS, BLOCK), F32),
            pltpu.VMEM((BLOCKS * HEADS, BLOCK), F32),
            pltpu.VMEM((BLOCKS, 2 * HEADS, BLOCK), BF16),
            pltpu.VMEM((BLOCKS, 2 * HEADS, BLOCK), BF16),
            pltpu.VMEM((2 * HEADS, COLS), BF16),
            pltpu.VMEM((32, COLS), F32),
            pltpu.VMEM((8, COLS), F32),
            pltpu.VMEM((STATE, WIDE), F32),
            pltpu.VMEM((BLOCKS, STATE, COLS), BF16),
            pltpu.VMEM((ROWS, COLS), F32),
            pltpu.VMEM((ROWS, COLS), BF16),
            pltpu.VMEM((BLOCK, COLS), F32),
            pltpu.VMEM((PARTS, STATE, WIDE), BF16),
            pltpu.VMEM((PARTS, ZS, SLICE, WIDE), BF16),
            pltpu.VMEM((PARTS, ZS, SLICE, WIDE), F32),
            pltpu.VMEM((PARTS, SLICE, WIDE), BF16),
            pltpu.VMEM((PARTS, XS, SLICE, WIDE), BF16),
            pltpu.VMEM((PARTS, ZS, SLICE, WIDE), BF16),
            pltpu.VMEM((PARTS, STATE, WIDE), BF16),
            pltpu.VMEM((8, 128), F32),
            pltpu.VMEM((ZS, 8, 128), F32),
            pltpu.VMEM((8, 128), F32),
            pltpu.VMEM((XS, 8, 128), F32),
            pltpu.VMEM((2 * ZS, COLS), F32),
            pltpu.VMEM((8, COLS), F32),
            dma((3 + PARTS,)),
            dma((2,)), dma((2,)),
            dma((ZS,)), dma((ZS,)),
            dma((XS,)), dma((XS,)),
            dma((PARTS, ZS)), dma((PARTS, ZS)),
            dma((PARTS, XS)), dma((PARTS, XS)),
            dma((PARTS, ZS)), dma((PARTS, ZS)),
            dma((24,)), dma((8, 3)), dma((3,)),
        ],
        compiler_params=pltpu.CompilerParams(
            collective_id=0, has_side_effects=True, vmem_limit_bytes=56 * 2**20
        ),
    )(
        channels_in,
        state_maps.reshape(ROWS, 2 * STATE),
        gate_in,
        step_raw,
        convolution_channel_taps,
        conv_maps.reshape(TAPS, 2 * STATE),
        head_rates,
        skip_gain.reshape(1, HEADS),
        norm_gain.reshape(1, COLS),
    )


def solution(mesh):
    return jax.shard_map(
        per_device,
        mesh=mesh,
        in_specs=(
            P("ctx", "head"),
            P("ctx", None, "head"),
            P("ctx", "head"),
            P("ctx", "head"),
            P(None, "head"),
            P(None, None, "head"),
            P(None, "head"),
            P("head"),
            P("head"),
        ),
        out_specs=P(("ctx", "head"), None),
        check_vma=False,
    )
```

```python
import jax
import jax.numpy as jnp
from jax import lax
from jax.experimental import pallas as pl
from jax.experimental.pallas import tpu as pltpu
from jax.sharding import PartitionSpec as P

HEAD_DIM = 64
STATE = 128
TAPS = 4
EPSILON = 1e-05
HI = lax.Precision.HIGHEST
MESH = pl.DeviceIdType.MESH
F32 = jnp.float32
BF16 = jnp.bfloat16

ROWS = 1536
COLS = 1024
HEADS = 16
BLOCK = 128
BLOCKS = ROWS // BLOCK
PARTS = 8
WIDE = COLS // PARTS
ZS = 8
XS = 4
SLICE = STATE // ZS
LEAD = 16
TARGET = ROWS // 8
PER = WIDE // HEAD_DIM
PASS = 3


def iota(shape, dim):
    return lax.broadcasted_iota(jnp.int32, shape, dim)


def dot(a, b, precision=None):
    return jnp.dot(a, b, precision=precision, preferred_element_type=F32)


def silu(v):
    half = 0.5 * v
    return half + half * jnp.tanh(half)


def split_in_two(v):
    high = v.astype(BF16).astype(F32)
    return high, v - high


def kernel(
    ch_hbm, bc_hbm, gate_hbm, step_hbm, taps, map_taps, rates, skip, gain, out,
    ch, bc, gate, step, wide, xs, bs, bt, cs, cum_v, step_v, tails, columns, spread,
    rows_v, skip_v, first_v, entering, scores_v, y0, squares, staged, landed,
    zs, z1, prefix, xt, x1, back, base, dl, dl_in, tl, tl_in, za, xa, scale_v, scale_in, scale_w,
    in_sem, halo_s, halo_r, dl_s, dl_r, tl_s, tl_r, z1_s, z1_r, x1_s, x1_r, z2_s, z2_r,
    y_s, y_r, own_sem, n_s, n_r,
):
    c = lax.axis_index("ctx")
    me = lax.axis_index("head")
    x, z = c // ZS, c % ZS
    y, core = me // 2, me % 2

    rest = pl.ds(WIDE, COLS - WIDE)
    loads = [
        pltpu.make_async_copy(step_hbm, step, in_sem.at[0]),
        pltpu.make_async_copy(bc_hbm, bc.at[pl.ds(LEAD, ROWS)], in_sem.at[1]),
        pltpu.make_async_copy(ch_hbm.at[:, pl.ds(0, WIDE)], ch.at[pl.ds(LEAD, ROWS), pl.ds(0, WIDE)], in_sem.at[2]),
        pltpu.make_async_copy(ch_hbm.at[:, rest], ch.at[pl.ds(LEAD, ROWS), rest], in_sem.at[3]),
        pltpu.make_async_copy(gate_hbm, gate, in_sem.at[4]),
    ]
    for load in loads[:3]:
        load.start()

    def z_peer(d):
        return (x * ZS + (z + d) % ZS, me)

    def x_peer(d):
        return (((x + d) % XS) * ZS + z, me)

    after, before = ((c + 1) % (XS * ZS), me), ((c + XS * ZS - 1) % (XS * ZS), me)
    peers = [z_peer(d) for d in range(1, ZS)] + [x_peer(d) for d in range(1, XS)]
    peers += [(c, (me + d) % 8) for d in range(1, 8)] + [after, before]
    barrier = pltpu.get_barrier_semaphore()
    for peer in peers:
        pl.semaphore_signal(barrier, inc=1, device_id=peer, device_id_type=MESH)

    spread[...] = (iota((2 * HEADS, COLS), 0) % HEADS == iota((2 * HEADS, COLS), 1) // HEAD_DIM).astype(BF16)
    head_of = (iota((HEADS, COLS), 0) == iota((HEADS, COLS), 1) // HEAD_DIM).astype(F32)
    bias = jnp.broadcast_to(rates[0:1, :], (BLOCK, HEADS)).T
    rate = jnp.broadcast_to(jnp.exp(rates[1:2, :]), (BLOCK, HEADS)).T
    rate = jnp.concatenate([rate] * BLOCKS, 0)
    loads[0].wait()
    raw = jnp.concatenate([step[:, pl.ds(k * BLOCK, BLOCK)] + bias for k in range(BLOCKS)], 0)
    sizes = jnp.maximum(raw, 0.0) + jnp.log1p(jnp.exp(-jnp.abs(raw)))
    logs = -rate * sizes
    row, col = iota((BLOCK, BLOCK), 0), iota((BLOCK, BLOCK), 1)
    cum = dot(logs, (row <= col).astype(F32), HI)
    later = dot(logs, (row > col).astype(F32), HI)
    cum_v[...] = cum
    step_v[...] = sizes
    high, low = split_in_two(jnp.exp(later) * sizes)
    for k in range(BLOCKS):
        of = slice(k * HEADS, (k + 1) * HEADS)
        tails[k] = jnp.concatenate([high[of], low[of]], 0).T.astype(BF16)
    count = BLOCKS * HEADS
    own_head = (iota((count, HEADS), 0) % HEADS == iota((count, HEADS), 1)).astype(F32)
    own_block = (iota((16, count), 0) == iota((16, count), 1) // HEADS).astype(F32)
    totals = dot(own_block, cum[:, BLOCK - 1 : BLOCK] * own_head, HI)
    row, col = iota((16, 16), 0), iota((16, 16), 1)
    earlier = dot(((row > col) & (col > 0)).astype(F32), totals, HI)
    growth = jnp.exp(dot(jnp.concatenate([totals, earlier], 0), head_of, HI))
    for q in range(PARTS):
        rows_v[q] = growth[:, q * WIDE : (q + 1) * WIDE]
    skip_v[...] = dot(jnp.broadcast_to(skip[...], (8, HEADS)), head_of, HI)
    whole = jnp.broadcast_to(earlier[BLOCKS : BLOCKS + 1] + totals[0:1], (8, HEADS))
    dl[...] = dot(whole, (iota((HEADS, 128), 0) == iota((HEADS, 128), 1)).astype(F32), HI)

    pl.semaphore_wait(barrier, len(peers))
    halo = [
        pltpu.make_async_remote_copy(
            src_ref=source.at[pl.ds(ROWS - LEAD, LEAD)], dst_ref=held.at[pl.ds(0, LEAD)],
            send_sem=halo_s.at[i], recv_sem=halo_r.at[i], device_id=after, device_id_type=MESH,
        )
        for i, (source, held) in enumerate(((bc_hbm, bc), (ch_hbm, ch)))
    ]
    for copy in halo:
        copy.start()
    dl_in[z] = dl[...]
    dl_copies = [
        pltpu.make_async_remote_copy(
            src_ref=dl, dst_ref=dl_in.at[z], send_sem=dl_s.at[d], recv_sem=dl_r.at[d],
            device_id=z_peer(d), device_id_type=MESH,
        )
        for d in range(1, ZS)
    ]
    for copy in dl_copies:
        copy.start()
    for load in loads[3:]:
        load.start()

    def conv(held, start, weight):
        total = weight(0) * held[pl.ds(start + LEAD - 3, BLOCK), :]
        for tap in range(1, TAPS):
            total += weight(tap) * held[pl.ds(start + LEAD - 3 + tap, BLOCK), :]
        return silu(total)

    def maps(k):
        start = k * BLOCK
        rows = pl.ds(start, BLOCK)
        b = conv(wide.at[0], start, lambda tap: map_taps[tap, 0:1, :])
        bs[rows, :] = b.astype(BF16)
        bt[k] = b.T.astype(BF16)
        c_map = conv(wide.at[1], start, lambda tap: map_taps[tap, 1:2, :]).astype(BF16)
        cs[rows, :STATE] = c_map
        cs[rows, STATE:] = c_map

    body, lead = pl.ds(LEAD, ROWS), pl.ds(0, LEAD)
    loads[1].wait()
    for i in range(2):
        wide[i, body, :] = bc[body, pl.ds(i * STATE, STATE)].astype(F32)
    for k in range(1, BLOCKS):
        maps(k)

    def lanes_of(q):
        return pl.ds(pl.multiple_of(q * WIDE, WIDE), WIDE)

    def summary(q, k):
        part = lanes_of(q)
        weights = dot(tails[k], spread[:, part])
        value = conv(wide.at[2], k * BLOCK, lambda tap: taps[tap : tap + 1, part]).astype(BF16)
        xs[q, pl.ds(k * BLOCK, BLOCK), :] = value
        return dot(bt[k], (value.astype(F32) * weights).astype(BF16))

    def blocks_but_first(q):
        part = lanes_of(q)
        wide[2, body, :] = ch[body, part].astype(F32)
        state = jnp.zeros((STATE, WIDE), F32)
        entering[q, 0] = state
        for k in range(1, BLOCKS):
            entering[q, k] = state
            state = rows_v[q, k : k + 1, :] * state + summary(q, k)
        zs[q] = state

    mine = pl.ds(pl.multiple_of(z * SLICE, SLICE), SLICE)

    def z1_copies(q):
        copies = []
        for d in (4, 3, 5, 2, 6, 1, 7):
            there = pl.ds(pl.multiple_of(((z + d) % ZS) * SLICE, SLICE), SLICE)
            copies.append(
                pltpu.make_async_remote_copy(
                    src_ref=xt.at[q, there], dst_ref=z1.at[q, z], send_sem=z1_s.at[q, d],
                    recv_sem=z1_r.at[q, d], device_id=z_peer(d), device_id_type=MESH,
                )
            )
        return copies

    def x1_copies(q):
        return [
            pltpu.make_async_remote_copy(
                src_ref=x1.at[q, x], dst_ref=x1.at[q, x], send_sem=x1_s.at[q, d],
                recv_sem=x1_r.at[q, d], device_id=x_peer(d), device_id_type=MESH,
            )
            for d in (2, 1, 3)
        ]

    def z2_copies(q):
        return [
            pltpu.make_async_remote_copy(
                src_ref=back.at[q, (z + d) % ZS], dst_ref=base.at[q, 0, mine], send_sem=z2_s.at[q, d],
                recv_sem=z2_r.at[q, d], device_id=z_peer(d), device_id_type=MESH,
            )
            for d in (4, 3, 5, 2, 6, 1, 7)
        ]

    def first_block(q):
        part = lanes_of(q)
        wide[2, lead, :] = ch[lead, part].astype(F32)
        first = summary(q, 0)
        first_v[q] = first
        state = (zs[q] + rows_v[q, 16 + BLOCKS : 17 + BLOCKS, :] * first).astype(BF16)
        xt[q] = state
        z1[q, z] = xt[q, mine, :]
        for copy in z1_copies(q):
            copy.start()

    def shard_decays():
        for copy in dl_copies:
            copy.wait()
        each = jnp.concatenate([dl_in[i, 0:1, :] for i in range(ZS)], 0)
        ahead = dot((iota((ZS, ZS), 0) > iota((ZS, ZS), 1)).astype(F32), each, HI)
        both = jnp.concatenate([each, ahead], 0)
        za[...] = jnp.exp(dot(both[:, :HEADS], head_of, HI))
        tl[...] = jnp.broadcast_to(jnp.sum(each, 0, keepdims=True), (8, 128))
        tl_in[x] = tl[...]
        copies = [
            pltpu.make_async_remote_copy(
                src_ref=tl, dst_ref=tl_in.at[x], send_sem=tl_s.at[d], recv_sem=tl_r.at[d],
                device_id=x_peer(d), device_id_type=MESH,
            )
            for d in range(1, XS)
        ]
        for copy in copies:
            copy.start()
        return copies

    def ring_decays(copies):
        for copy in copies:
            copy.wait()
        each = jnp.concatenate([tl_in[i, 0:1, :] for i in range(XS)] * 2, 0)
        xa[...] = jnp.exp(dot(each[:, :HEADS], head_of, HI))

    def along_z(q):
        part = lanes_of(q)
        for copy in z1_copies(q):
            copy.wait()
        total = jnp.zeros((SLICE, WIDE), F32)
        for i in range(ZS):
            prefix[q, i] = total
            total = za[i : i + 1, part] * total + z1[q, i].astype(F32)
        x1[q, x] = total
        for copy in x1_copies(q):
            copy.start()

    def along_x(q):
        part = lanes_of(q)
        for copy in x1_copies(q):
            copy.wait()
        total = jnp.zeros((SLICE, WIDE), F32)
        for i in range(XS - 1):
            total = jnp.where(i < x, xa[i : i + 1, part] * total + x1[q, i], total)
        for i in range(ZS):
            back[q, i] = prefix[q, i] + za[ZS + i : ZS + i + 1, part] * total
        base[q, 0, mine, :] = back[q, z]
        for copy in z2_copies(q):
            copy.start()

    def blocks_alone():
        @pl.loop(0, BLOCKS)
        def _(k):
            rows = pl.ds(pl.multiple_of(k * BLOCK, BLOCK), BLOCK)
            scores = lax.dot_general(
                cs[rows, :STATE], bs[rows, :], (((1,), (1,)), ((), ())), preferred_element_type=F32
            )
            scores_v[k] = jnp.where(iota((BLOCK, BLOCK), 0) >= iota((BLOCK, BLOCK), 1), scores, 0.0)
            sums = cum_v[pl.ds(pl.multiple_of(k * HEADS, HEADS), HEADS), :]
            high, low = split_in_two(sums)
            middle, low = split_in_two(low)
            parts = [high, middle, low, *split_in_two(jnp.exp(sums))]
            columns[k] = jnp.concatenate(parts, 0).T.astype(BF16)

    def inside(q):
        part = lanes_of(q)
        left = iota((BLOCK, WIDE), 1) < HEAD_DIM
        pick = PER * q + iota((3 * HEADS, PER * BLOCK), 1) // BLOCK == iota((3 * HEADS, PER * BLOCK), 0) % HEADS
        pick = pick.astype(BF16)

        @pl.loop(0, BLOCKS // 3)
        def _(j):
            for i in range(3):
                k = 3 * j + i
                rows = pl.ds(pl.multiple_of(k * BLOCK, BLOCK), BLOCK)
                down = dot(columns[k, :, : 3 * HEADS], pick)
                weights = []
                for h in range(PER):
                    at = pl.ds(k * HEADS + PER * q + h, 1)
                    gap = jnp.minimum(down[:, h * BLOCK : (h + 1) * BLOCK] - cum_v[at, :], 0.0)
                    weights.append((scores_v[k] * jnp.exp(gap) * step_v[at, :]).astype(BF16))
                value = xs[q, rows, :]
                none = jnp.zeros_like(value)
                both = jnp.concatenate([jnp.where(left, value, none), jnp.where(left, none, value)], 0)
                y0[rows, :] = dot(jnp.concatenate(weights, 1), both) + skip_v[0:1, part] * value.astype(F32)

    def send_of(q, t, to):
        delta = (t * t + t + 1) % 5 * (1 - t // 3)
        there = (y + delta) % 4
        return pltpu.make_async_remote_copy(
            src_ref=staged.at[q, pl.ds(pl.multiple_of((2 * there + to) * TARGET, TARGET), TARGET)],
            dst_ref=landed.at[me, q], send_sem=y_s.at[q, t, to], recv_sem=y_r.at[q, me],
            device_id=(c, 2 * there + to), device_id_type=MESH,
        )

    def own_of(q):
        return pltpu.make_async_copy(
            staged.at[q, pl.ds(pl.multiple_of(me * TARGET, TARGET), TARGET)],
            landed.at[me, q], own_sem.at[q],
        )

    def scale_of(t, to):
        delta = (t * t + t + 1) % 5 * (1 - t // 3)
        there = (y + delta) % 4
        return pltpu.make_async_remote_copy(
            src_ref=scale_v.at[there], dst_ref=scale_in.at[me], send_sem=n_s.at[t, to],
            recv_sem=n_r.at[me], device_id=(c, 2 * there + to), device_id_type=MESH,
        )

    def all_but_own(t, to, remote, own):
        @pl.when((t < 3) | (to != core))
        def _():
            remote()

        @pl.when((t == 3) & (to == core))
        def _():
            own()

    def finish(q):
        part = lanes_of(q)
        for copy in z2_copies(q):
            copy.wait()
        base[q, 1] = rows_v[q, 0:1, :] * base[q, 0] + first_v[q]

        @pl.loop(0, 4)
        def _(t):
            delta = (t * t + t + 1) % 5 * (1 - t // 3)
            there = (y + delta) % 4
            for m in range(PASS):
                k = PASS * there + m
                rows = pl.ds(pl.multiple_of(k * BLOCK, BLOCK), BLOCK)
                state_in = entering[q, k] + rows_v[q, pl.ds(16 + k, 1), :] * base[q, jnp.minimum(k, 1)]
                high, low = split_in_two(state_in)
                from_state = dot(cs[rows, :], jnp.concatenate([high, low], 0).astype(BF16))
                decay = dot(columns[k, :, 3 * HEADS :], spread[:, part])
                value = (y0[rows, :] + decay * from_state) * silu(gate[rows, part].astype(F32))
                square = jnp.where(q == 0, 0.0, squares[rows, :]) + value * value
                squares[rows, :] = square
                staged[q, rows, :] = (value * gain[0:1, part]).astype(BF16)
                if m > 0:
                    to = m - 1
                    all_but_own(t, to, send_of(q, t, to).start, own_of(q).start)

    def scales():
        @pl.loop(0, 4)
        def _(t):
            delta = (t * t + t + 1) % 5 * (1 - t // 3)
            there = (y + delta) % 4
            for m in range(PASS):
                rows = pl.ds(pl.multiple_of((PASS * there + m) * BLOCK, BLOCK), BLOCK)
                scale = lax.rsqrt(jnp.sum(squares[rows, :], 1, keepdims=True) / COLS + EPSILON)
                scale_v[there, m] = jnp.broadcast_to(scale, (BLOCK, 128)).T[0:8, :]
            for to in range(2):

                def own():
                    scale_in[me] = scale_v[there]

                all_but_own(t, to, scale_of(t, to).start, own)

    loads[2].wait()
    blocks_but_first(0)
    for copy in halo:
        copy.wait()

    @pl.when(c == 0)
    def _():
        bc[lead, :] = jnp.zeros((LEAD, 2 * STATE), BF16)
        ch[lead, :] = jnp.zeros((LEAD, COLS), BF16)

    for i in range(2):
        wide[i, lead, :] = bc[lead, pl.ds(i * STATE, STATE)].astype(F32)
    maps(0)
    first_block(0)
    loads[3].wait()

    def steps(low, high, *more):
        @pl.loop(low, high)
        def _(q):
            blocks_but_first(q)
            first_block(q)
            for what, lag in more:
                what(q - lag)

    steps(1, 3)
    rings = shard_decays()
    steps(3, 5, (along_z, 3))
    ring_decays(rings)
    steps(5, PARTS, (along_z, 3), (along_x, 5))
    blocks_alone()
    loads[4].wait()

    @pl.loop(0, PARTS)
    def _(q):
        inside(q)
        finish(q)

        @pl.when(q < 3)
        def _():
            along_z(q + PARTS - 3)

        @pl.when(q < 5)
        def _():
            along_x(q + PARTS - 5)

    scales()

    def place(source):
        for m in range(PASS):
            scale_w[pl.ds(m * BLOCK, BLOCK), :] = jnp.broadcast_to(scale_in[source, m, 0:1, :], (128, BLOCK)).T
        scale = scale_w[pl.ds(pl.multiple_of(core * TARGET, TARGET), TARGET), :]
        for q in range(PARTS):
            lanes = pl.ds(pl.multiple_of(source * COLS + q * WIDE, WIDE), WIDE)
            out[:, lanes] = (landed[source, q].astype(F32) * scale).astype(BF16)

    for q in range(PARTS):
        own_of(q).wait()
    place(me)

    @pl.loop(1, 8)
    def _(d):
        source = (me + d) % 8
        for q in range(PARTS):
            pltpu.make_async_remote_copy(
                src_ref=staged.at[q, pl.ds(0, TARGET)], dst_ref=landed.at[source, q],
                send_sem=y_s.at[q, 0, 0], recv_sem=y_r.at[q, source],
                device_id=(c, source), device_id_type=MESH,
            ).wait_recv()
        pltpu.make_async_remote_copy(
            src_ref=scale_v.at[0], dst_ref=scale_in.at[source], send_sem=n_s.at[0, 0],
            recv_sem=n_r.at[source], device_id=(c, source), device_id_type=MESH,
        ).wait_recv()
        place(source)

    @pl.loop(0, 4)
    def _(t):
        for to in range(2):

            def remote():
                for q in range(PARTS):
                    send_of(q, t, to).wait_send()
                scale_of(t, to).wait_send()

            all_but_own(t, to, remote, lambda: None)


def per_device(
    channels_in,
    state_maps,
    gate_in,
    step_raw,
    convolution_channel_taps,
    conv_maps,
    head_rates,
    skip_gain,
    norm_gain,
):
    anywhere = pl.BlockSpec(memory_space=pl.ANY)
    near = pl.BlockSpec(memory_space=pltpu.VMEM)
    dma = pltpu.SemaphoreType.DMA
    return pl.pallas_call(
        kernel,
        out_shape=pltpu.VMEM((TARGET, COLS * 8), BF16),
        in_specs=[anywhere] * 4 + [near] * 5,
        out_specs=near,
        scratch_shapes=[
            pltpu.VMEM((LEAD + ROWS, COLS), BF16),
            pltpu.VMEM((LEAD + ROWS, 2 * STATE), BF16),
            pltpu.VMEM((ROWS, COLS), BF16),
            pltpu.VMEM((HEADS, ROWS), F32),
            pltpu.VMEM((3, LEAD + ROWS, 128), F32),
            pltpu.VMEM((PARTS, ROWS, WIDE), BF16),
            pltpu.VMEM((ROWS, STATE), BF16),
            pltpu.VMEM((BLOCKS, STATE, BLOCK), BF16),
            pltpu.VMEM((ROWS, 2 * STATE), BF16),
            pltpu.VMEM((BLOCKS * HEADS, BLOCK), F32),
            pltpu.VMEM((BLOCKS * HEADS, BLOCK), F32),
            pltpu.VMEM((BLOCKS, BLOCK, 2 * HEADS), BF16),
            pltpu.VMEM((BLOCKS, BLOCK, 5 * HEADS), BF16),
            pltpu.VMEM((2 * HEADS, COLS), BF16),
            pltpu.VMEM((PARTS, 32, WIDE), F32),
            pltpu.VMEM((8, COLS), F32),
            pltpu.VMEM((PARTS, STATE, WIDE), F32),
            pltpu.VMEM((PARTS, BLOCKS, STATE, WIDE), F32),
            pltpu.VMEM((BLOCKS, BLOCK, BLOCK), F32),
            pltpu.VMEM((ROWS, WIDE), F32),
            pltpu.VMEM((ROWS, WIDE), F32),
            pltpu.VMEM((PARTS, ROWS, WIDE), BF16),
            pltpu.VMEM((8, PARTS, TARGET, WIDE), BF16),
            pltpu.VMEM((PARTS, STATE, WIDE), F32),
            pltpu.VMEM((PARTS, ZS, SLICE, WIDE), BF16),
            pltpu.VMEM((PARTS, ZS, SLICE, WIDE), F32),
            pltpu.VMEM((PARTS, STATE, WIDE), BF16),
            pltpu.VMEM((PARTS, XS, SLICE, WIDE), F32),
            pltpu.VMEM((PARTS, ZS, SLICE, WIDE), F32),
            pltpu.VMEM((PARTS, 2, STATE, WIDE), F32),
            pltpu.VMEM((8, 128), F32),
            pltpu.VMEM((ZS, 8, 128), F32),
            pltpu.VMEM((8, 128), F32),
            pltpu.VMEM((XS, 8, 128), F32),
            pltpu.VMEM((2 * ZS, COLS), F32),
            pltpu.VMEM((8, COLS), F32),
            pltpu.VMEM((4, PASS, 8, BLOCK), F32),
            pltpu.VMEM((8, PASS, 8, BLOCK), F32),
            pltpu.VMEM((PASS * BLOCK, 128), F32),
            dma((5,)),
            dma((2,)), dma((2,)),
            dma((ZS,)), dma((ZS,)),
            dma((XS,)), dma((XS,)),
            dma((PARTS, ZS)), dma((PARTS, ZS)),
            dma((PARTS, XS)), dma((PARTS, XS)),
            dma((PARTS, ZS)), dma((PARTS, ZS)),
            dma((PARTS, 4, 2)), dma((PARTS, 8)), dma((PARTS,)),
            dma((4, 2)), dma((8,)),
        ],
        compiler_params=pltpu.CompilerParams(
            collective_id=0, has_side_effects=True, vmem_limit_bytes=60 * 2**20
        ),
    )(
        channels_in,
        state_maps.reshape(ROWS, 2 * STATE),
        gate_in,
        step_raw.T,
        convolution_channel_taps,
        conv_maps,
        head_rates,
        skip_gain.reshape(1, HEADS),
        norm_gain.reshape(1, COLS),
    )


def solution(mesh):
    return jax.shard_map(
        per_device,
        mesh=mesh,
        in_specs=(
            P("ctx", "head"),
            P("ctx", None, "head"),
            P("ctx", "head"),
            P("ctx", "head"),
            P(None, "head"),
            P(None, None, "head"),
            P(None, "head"),
            P("head"),
            P("head"),
        ),
        out_specs=P(("ctx", "head"), None),
        check_vma=False,
    )
```

```python
import jax
import jax.numpy as jnp
from jax import lax
from jax.experimental import pallas as pl
from jax.experimental.pallas import tpu as pltpu
from jax.sharding import PartitionSpec as P

HEAD_DIM = 64
STATE = 128
TAPS = 4
EPSILON = 1e-05
HI = lax.Precision.HIGHEST
MESH = pl.DeviceIdType.MESH
F32 = jnp.float32
BF16 = jnp.bfloat16

ROWS = 1536
COLS = 1024
HEADS = 16
BLOCK = 128
BLOCKS = ROWS // BLOCK
PARTS = 8
WIDE = COLS // PARTS
ZS = 8
XS = 4
SLICE = STATE // ZS
LEAD = 16
TARGET = ROWS // 8
PER = WIDE // HEAD_DIM
PASS = 3
HELD = 2


def iota(shape, dim):
    return lax.broadcasted_iota(jnp.int32, shape, dim)


def dot(a, b, precision=None):
    return jnp.dot(a, b, precision=precision, preferred_element_type=F32)


def silu(v):
    half = 0.5 * v
    return half + half * jnp.tanh(half)


def split_in_two(v):
    high = v.astype(BF16).astype(F32)
    return high, v - high


def kernel(
    ch_hbm, bc_hbm, gate_hbm, step_hbm, taps, map_taps, rates, skip, gain, out,
    ch, bc, gate, step, wide, wide_maps, xs, bs, bt, cs, cum_v, step_v, tails, columns, spread,
    rows_v, skip_v, first_v, entering, scores_v, y0, squares, staged, landed,
    zs, z1, prefix, xt, x1, back, base, dl, dl_in, tl, tl_in, za, xa, scale_v, scale_in, scale_w, scale_all,
    in_sem, halo_s, halo_r, dl_s, dl_r, tl_s, tl_r, z1_s, z1_r, x1_s, x1_r, z2_s, z2_r,
    y_s, y_r, own_sem, n_s, n_r,
):
    c = lax.axis_index("ctx")
    me = lax.axis_index("head")
    x, z = c // ZS, c % ZS
    y, core = me // 2, me % 2

    rest = pl.ds(WIDE, COLS - WIDE)
    loads = [
        pltpu.make_async_copy(step_hbm, step, in_sem.at[0]),
        pltpu.make_async_copy(bc_hbm, bc.at[pl.ds(2 * LEAD, 2 * ROWS)], in_sem.at[1]),
        pltpu.make_async_copy(ch_hbm.at[:, pl.ds(0, WIDE)], ch.at[pl.ds(LEAD, ROWS), pl.ds(0, WIDE)], in_sem.at[2]),
        pltpu.make_async_copy(ch_hbm.at[:, rest], ch.at[pl.ds(LEAD, ROWS), rest], in_sem.at[3]),
        pltpu.make_async_copy(gate_hbm, gate, in_sem.at[4]),
    ]
    for load in loads[:3]:
        load.start()

    def z_peer(d):
        return (x * ZS + (z + d) % ZS, me)

    def x_peer(d):
        return (((x + d) % XS) * ZS + z, me)

    after, before = ((c + 1) % (XS * ZS), me), ((c + XS * ZS - 1) % (XS * ZS), me)
    peers = [z_peer(d) for d in range(1, ZS)] + [x_peer(d) for d in range(1, XS)]
    peers += [(c, (me + d) % 8) for d in range(1, 8)] + [after, before]
    barrier = pltpu.get_barrier_semaphore()
    for peer in peers:
        pl.semaphore_signal(barrier, inc=1, device_id=peer, device_id_type=MESH)

    spread[...] = (iota((2 * HEADS, COLS), 0) % HEADS == iota((2 * HEADS, COLS), 1) // HEAD_DIM).astype(BF16)
    head_of = (iota((HEADS, COLS), 0) == iota((HEADS, COLS), 1) // HEAD_DIM).astype(F32)
    bias = jnp.broadcast_to(rates[0:1, :], (BLOCK, HEADS)).T
    rate = jnp.broadcast_to(jnp.exp(rates[1:2, :]), (BLOCK, HEADS)).T
    rate = jnp.concatenate([rate] * BLOCKS, 0)
    loads[0].wait()
    raw = jnp.concatenate([step[:, pl.ds(k * BLOCK, BLOCK)] + bias for k in range(BLOCKS)], 0)
    sizes = jnp.maximum(raw, 0.0) + jnp.log1p(jnp.exp(-jnp.abs(raw)))
    logs = -rate * sizes
    row, col = iota((BLOCK, BLOCK), 0), iota((BLOCK, BLOCK), 1)
    cum = dot(logs, (row <= col).astype(F32), HI)
    later = dot(logs, (row > col).astype(F32), HI)
    cum_v[...] = cum
    step_v[...] = sizes
    high, low = split_in_two(jnp.exp(later) * sizes)
    for k in range(BLOCKS):
        of = slice(k * HEADS, (k + 1) * HEADS)
        tails[k] = jnp.concatenate([high[of], low[of]], 0).T.astype(BF16)
    count = BLOCKS * HEADS
    own_head = (iota((count, HEADS), 0) % HEADS == iota((count, HEADS), 1)).astype(F32)
    own_block = (iota((16, count), 0) == iota((16, count), 1) // HEADS).astype(F32)
    totals = dot(own_block, cum[:, BLOCK - 1 : BLOCK] * own_head, HI)
    row, col = iota((16, 16), 0), iota((16, 16), 1)
    earlier = dot(((row > col) & (col > 0)).astype(F32), totals, HI)
    growth = jnp.exp(dot(jnp.concatenate([totals, earlier], 0), head_of, HI))
    for q in range(PARTS):
        rows_v[q] = growth[:, q * WIDE : (q + 1) * WIDE]
    skip_v[...] = dot(jnp.broadcast_to(skip[...], (8, HEADS)), head_of, HI)
    whole = jnp.broadcast_to(earlier[BLOCKS : BLOCKS + 1] + totals[0:1], (8, HEADS))
    dl[...] = dot(whole, (iota((HEADS, 128), 0) == iota((HEADS, 128), 1)).astype(F32), HI)

    pl.semaphore_wait(barrier, len(peers))
    ends = [
        (bc_hbm.at[pl.ds(2 * (ROWS - LEAD), 2 * LEAD)], bc.at[pl.ds(0, 2 * LEAD)]),
        *((ch_hbm.at[pl.ds(ROWS - LEAD, LEAD), at], ch.at[pl.ds(0, LEAD), at]) for at in (pl.ds(0, WIDE), rest)),
    ]
    halo = [
        pltpu.make_async_remote_copy(
            src_ref=source, dst_ref=held, send_sem=halo_s.at[i], recv_sem=halo_r.at[i],
            device_id=after, device_id_type=MESH,
        )
        for i, (source, held) in enumerate(ends)
    ]
    for copy in halo[:2]:
        copy.start()
    dl_in[z] = dl[...]
    dl_copies = [
        pltpu.make_async_remote_copy(
            src_ref=dl, dst_ref=dl_in.at[z], send_sem=dl_s.at[d], recv_sem=dl_r.at[d],
            device_id=z_peer(d), device_id_type=MESH,
        )
        for d in range(1, ZS)
    ]
    for copy in dl_copies:
        copy.start()
    halo[2].start()
    for load in loads[3:]:
        load.start()

    def conv(row, weight):
        total = weight(0) * row(LEAD - 3)
        for tap in range(1, TAPS):
            total += weight(tap) * row(LEAD - 3 + tap)
        return silu(total)

    def maps(k):
        rows = pl.ds(k * BLOCK, BLOCK)

        def each(i):
            return conv(
                lambda r: wide_maps[pl.ds(2 * (k * BLOCK + r) + i, BLOCK, stride=2), :],
                lambda tap: map_taps[tap, i : i + 1, :],
            )

        b = each(0)
        bs[rows, :] = b.astype(BF16)
        bt[k] = b.T.astype(BF16)
        c_map = each(1).astype(BF16)
        cs[rows, :STATE] = c_map
        cs[rows, STATE:] = c_map

    body, lead = pl.ds(LEAD, ROWS), pl.ds(0, LEAD)
    loads[1].wait()
    wide_maps[pl.ds(2 * LEAD, 2 * ROWS), :] = bc[pl.ds(2 * LEAD, 2 * ROWS), :].astype(F32)
    for k in range(1, BLOCKS):
        maps(k)

    def lanes_of(q):
        return pl.ds(pl.multiple_of(q * WIDE, WIDE), WIDE)

    def summary(q, k):
        part = lanes_of(q)
        weights = dot(tails[k], spread[:, part])
        value = conv(
            lambda r: wide[pl.ds(k * BLOCK + r, BLOCK), :], lambda tap: taps[tap : tap + 1, part]
        ).astype(BF16)
        xs[q, pl.ds(k * BLOCK, BLOCK), :] = value
        return dot(bt[k], (value.astype(F32) * weights).astype(BF16))

    def blocks_but_first(q):
        part = lanes_of(q)
        wide[body, :] = ch[body, part].astype(F32)
        state = jnp.zeros((STATE, WIDE), F32)
        entering[q, 0] = state
        for k in range(1, BLOCKS):
            entering[q, k] = state
            state = rows_v[q, k : k + 1, :] * state + summary(q, k)
        zs[q] = state

    mine = pl.ds(pl.multiple_of(z * SLICE, SLICE), SLICE)

    def z1_copies(q):
        copies = []
        for d in (4, 3, 5, 2, 6, 1, 7):
            there = pl.ds(pl.multiple_of(((z + d) % ZS) * SLICE, SLICE), SLICE)
            copies.append(
                pltpu.make_async_remote_copy(
                    src_ref=xt.at[q, there], dst_ref=z1.at[q, z], send_sem=z1_s.at[q, d],
                    recv_sem=z1_r.at[q, d], device_id=z_peer(d), device_id_type=MESH,
                )
            )
        return copies

    def x1_copies(q):
        return [
            pltpu.make_async_remote_copy(
                src_ref=x1.at[q, x], dst_ref=x1.at[q, x], send_sem=x1_s.at[q, d],
                recv_sem=x1_r.at[q, d], device_id=x_peer(d), device_id_type=MESH,
            )
            for d in (2, 1, 3)
        ]

    def z2_copies(q):
        return [
            pltpu.make_async_remote_copy(
                src_ref=back.at[q, (z + d) % ZS], dst_ref=base.at[q, 0, mine], send_sem=z2_s.at[q, d],
                recv_sem=z2_r.at[q, d], device_id=z_peer(d), device_id_type=MESH,
            )
            for d in (4, 3, 5, 2, 6, 1, 7)
        ]

    def first_block(q):
        part = lanes_of(q)
        wide[lead, :] = ch[lead, part].astype(F32)
        first = summary(q, 0)
        first_v[q] = first
        state = (zs[q] + rows_v[q, 16 + BLOCKS : 17 + BLOCKS, :] * first).astype(BF16)
        xt[q] = state
        z1[q, z] = xt[q, mine, :]
        for copy in z1_copies(q):
            copy.start()

    def shard_decays():
        for copy in dl_copies:
            copy.wait()
        each = jnp.concatenate([dl_in[i, 0:1, :] for i in range(ZS)], 0)
        ahead = dot((iota((ZS, ZS), 0) > iota((ZS, ZS), 1)).astype(F32), each, HI)
        both = jnp.concatenate([each, ahead], 0)
        za[...] = jnp.exp(dot(both[:, :HEADS], head_of, HI))
        tl[...] = jnp.broadcast_to(jnp.sum(each, 0, keepdims=True), (8, 128))
        tl_in[x] = tl[...]
        copies = [
            pltpu.make_async_remote_copy(
                src_ref=tl, dst_ref=tl_in.at[x], send_sem=tl_s.at[d], recv_sem=tl_r.at[d],
                device_id=x_peer(d), device_id_type=MESH,
            )
            for d in range(1, XS)
        ]
        for copy in copies:
            copy.start()
        return copies

    def ring_decays(copies):
        for copy in copies:
            copy.wait()
        each = jnp.concatenate([tl_in[i, 0:1, :] for i in range(XS)] * 2, 0)
        xa[...] = jnp.exp(dot(each[:, :HEADS], head_of, HI))

    def along_z(q):
        part = lanes_of(q)
        for copy in z1_copies(q):
            copy.wait()
        total = jnp.zeros((SLICE, WIDE), F32)
        for i in range(ZS):
            prefix[q, i] = total
            total = za[i : i + 1, part] * total + z1[q, i].astype(F32)
        x1[q, x] = total
        for copy in x1_copies(q):
            copy.start()

    def along_x(q):
        part = lanes_of(q)
        for copy in x1_copies(q):
            copy.wait()
        total = jnp.zeros((SLICE, WIDE), F32)
        for i in range(XS - 1):
            total = jnp.where(i < x, xa[i : i + 1, part] * total + x1[q, i], total)
        for i in range(ZS):
            back[q, i] = prefix[q, i] + za[ZS + i : ZS + i + 1, part] * total
        base[q, 0, mine, :] = back[q, z]
        for copy in z2_copies(q):
            copy.start()

    def blocks_alone():
        @pl.loop(0, BLOCKS)
        def _(k):
            rows = pl.ds(pl.multiple_of(k * BLOCK, BLOCK), BLOCK)
            scores = lax.dot_general(
                cs[rows, :STATE], bs[rows, :], (((1,), (1,)), ((), ())), preferred_element_type=F32
            )
            scores_v[k] = jnp.where(iota((BLOCK, BLOCK), 0) >= iota((BLOCK, BLOCK), 1), scores, 0.0)
            sums = cum_v[pl.ds(pl.multiple_of(k * HEADS, HEADS), HEADS), :]
            high, low = split_in_two(sums)
            middle, low = split_in_two(low)
            parts = [high, middle, low, *split_in_two(jnp.exp(sums))]
            columns[k] = jnp.concatenate(parts, 0).T.astype(BF16)

    def inside(q):
        part = lanes_of(q)
        left = iota((BLOCK, WIDE), 1) < HEAD_DIM
        pick = PER * q + iota((3 * HEADS, PER * BLOCK), 1) // BLOCK == iota((3 * HEADS, PER * BLOCK), 0) % HEADS
        pick = pick.astype(BF16)

        @pl.loop(0, BLOCKS // 3)
        def _(j):
            for i in range(3):
                k = 3 * j + i
                rows = pl.ds(pl.multiple_of(k * BLOCK, BLOCK), BLOCK)
                down = dot(columns[k, :, : 3 * HEADS], pick)
                weights = []
                for h in range(PER):
                    at = pl.ds(k * HEADS + PER * q + h, 1)
                    gap = jnp.minimum(down[:, h * BLOCK : (h + 1) * BLOCK] - cum_v[at, :], 0.0)
                    weights.append((scores_v[k] * jnp.exp(gap) * step_v[at, :]).astype(BF16))
                value = xs[q, rows, :]
                none = jnp.zeros_like(value)
                both = jnp.concatenate([jnp.where(left, value, none), jnp.where(left, none, value)], 0)
                y0[rows, :] = dot(jnp.concatenate(weights, 1), both) + skip_v[0:1, part] * value.astype(F32)

    def send_of(q, t, to):
        delta = (t * t + t + 1) % 5 * (1 - t // 3)
        there = (y + delta) % 4
        return pltpu.make_async_remote_copy(
            src_ref=staged.at[q, pl.ds(pl.multiple_of((2 * there + to) * TARGET, TARGET), TARGET)],
            dst_ref=landed.at[me, q], send_sem=y_s.at[q, t, to], recv_sem=y_r.at[q, me],
            device_id=(c, 2 * there + to), device_id_type=MESH,
        )

    def own_of(q):
        return pltpu.make_async_copy(
            staged.at[q, pl.ds(pl.multiple_of(me * TARGET, TARGET), TARGET)],
            landed.at[me, q], own_sem.at[q],
        )

    def scale_of(t, to):
        delta = (t * t + t + 1) % 5 * (1 - t // 3)
        there = (y + delta) % 4
        return pltpu.make_async_remote_copy(
            src_ref=scale_v.at[there], dst_ref=scale_in.at[me], send_sem=n_s.at[t, to],
            recv_sem=n_r.at[me], device_id=(c, 2 * there + to), device_id_type=MESH,
        )

    def all_but_own(t, to, remote, own):
        @pl.when((t < 3) | (to != core))
        def _():
            remote()

        @pl.when((t == 3) & (to == core))
        def _():
            own()

    def ship(q, t, to):
        all_but_own(t, to, send_of(q, t, to).start, own_of(q).start)

    def finish(q, send):
        part = lanes_of(q)
        for copy in z2_copies(q):
            copy.wait()
        base[q, 1] = rows_v[q, 0:1, :] * base[q, 0] + first_v[q]

        @pl.loop(0, 4)
        def _(t):
            delta = (t * t + t + 1) % 5 * (1 - t // 3)
            there = (y + delta) % 4
            for m in range(PASS):
                k = PASS * there + m
                rows = pl.ds(pl.multiple_of(k * BLOCK, BLOCK), BLOCK)
                state_in = entering[q, k] + rows_v[q, pl.ds(16 + k, 1), :] * base[q, jnp.minimum(k, 1)]
                high, low = split_in_two(state_in)
                from_state = dot(cs[rows, :], jnp.concatenate([high, low], 0).astype(BF16))
                decay = dot(columns[k, :, 3 * HEADS :], spread[:, part])
                value = (y0[rows, :] + decay * from_state) * silu(gate[rows, part].astype(F32))
                square = jnp.where(q == 0, 0.0, squares[rows, :]) + value * value
                squares[rows, :] = square
                staged[q, rows, :] = (value * gain[0:1, part]).astype(BF16)
                if send and m > 0:
                    ship(q, t, m - 1)

    def scales():
        @pl.loop(0, 4)
        def _(t):
            delta = (t * t + t + 1) % 5 * (1 - t // 3)
            there = (y + delta) % 4
            for m in range(PASS):
                rows = pl.ds(pl.multiple_of((PASS * there + m) * BLOCK, BLOCK), BLOCK)
                scale = lax.rsqrt(jnp.sum(squares[rows, :], 1, keepdims=True) / COLS + EPSILON)
                scale_v[there, m] = jnp.broadcast_to(scale, (BLOCK, 128)).T[0:8, :]
            for to in range(2):

                def own():
                    scale_in[me] = scale_v[there]

                all_but_own(t, to, scale_of(t, to).start, own)

    loads[2].wait()
    blocks_but_first(0)
    for copy in halo[:2]:
        copy.wait()

    @pl.when(c == 0)
    def _():
        bc[pl.ds(0, 2 * LEAD), :] = jnp.zeros((2 * LEAD, STATE), BF16)
        ch[lead, pl.ds(0, WIDE)] = jnp.zeros((LEAD, WIDE), BF16)

    wide_maps[pl.ds(0, 2 * LEAD), :] = bc[pl.ds(0, 2 * LEAD), :].astype(F32)
    maps(0)
    first_block(0)
    loads[3].wait()
    halo[2].wait()

    @pl.when(c == 0)
    def _():
        ch[lead, rest] = jnp.zeros((LEAD, COLS - WIDE), BF16)

    def steps(low, high, *more):
        @pl.loop(low, high)
        def _(q):
            blocks_but_first(q)
            first_block(q)
            for what, lag in more:
                what(q - lag)

    steps(1, 3)
    rings = shard_decays()
    steps(3, 5, (along_z, 3))
    ring_decays(rings)
    steps(5, PARTS, (along_z, 3), (along_x, 5))
    blocks_alone()
    loads[4].wait()

    @pl.loop(0, PARTS - HELD)
    def _(q):
        inside(q)
        finish(q, True)

        @pl.when(q < 3)
        def _():
            along_z(q + PARTS - 3)

        @pl.when(q < 5)
        def _():
            along_x(q + PARTS - 5)

    for q in range(PARTS - HELD, PARTS):
        inside(q)
        finish(q, False)
    scales()

    @pl.loop(PARTS - HELD, PARTS)
    def _(q):
        @pl.loop(0, 4)
        def _(t):
            for to in range(2):
                ship(q, t, to)

    def spread_scale(source):
        for m in range(PASS):
            scale_w[pl.ds(m * BLOCK, BLOCK), :] = jnp.broadcast_to(scale_in[source, m, 0:1, :], (128, BLOCK)).T
        scale_all[source] = scale_w[pl.ds(pl.multiple_of(core * TARGET, TARGET), TARGET), :]

    def place(source, q):
        lanes = pl.ds(pl.multiple_of(source * COLS + q * WIDE, WIDE), WIDE)
        out[:, lanes] = (landed[source, q].astype(F32) * scale_all[source]).astype(BF16)

    spread_scale(me)

    @pl.loop(0, PARTS)
    def _(q):
        own_of(q).wait()
        place(me, q)

    @pl.loop(1, 8)
    def _(d):
        source = (me + d) % 8
        pltpu.make_async_remote_copy(
            src_ref=scale_v.at[0], dst_ref=scale_in.at[source], send_sem=n_s.at[0, 0],
            recv_sem=n_r.at[source], device_id=(c, source), device_id_type=MESH,
        ).wait_recv()
        spread_scale(source)

    @pl.loop(0, PARTS)
    def _(q):
        @pl.loop(1, 8)
        def _(d):
            source = (me + d) % 8
            pltpu.make_async_remote_copy(
                src_ref=staged.at[q, pl.ds(0, TARGET)], dst_ref=landed.at[source, q],
                send_sem=y_s.at[q, 0, 0], recv_sem=y_r.at[q, source],
                device_id=(c, source), device_id_type=MESH,
            ).wait_recv()
            place(source, q)

    @pl.loop(0, 4)
    def _(t):
        for to in range(2):

            def remote():
                for q in range(PARTS):
                    send_of(q, t, to).wait_send()
                scale_of(t, to).wait_send()

            all_but_own(t, to, remote, lambda: None)


def per_device(
    channels_in,
    state_maps,
    gate_in,
    step_raw,
    convolution_channel_taps,
    conv_maps,
    head_rates,
    skip_gain,
    norm_gain,
):
    anywhere = pl.BlockSpec(memory_space=pl.ANY)
    near = pl.BlockSpec(memory_space=pltpu.VMEM)
    dma = pltpu.SemaphoreType.DMA
    return pl.pallas_call(
        kernel,
        out_shape=pltpu.VMEM((TARGET, COLS * 8), BF16),
        in_specs=[anywhere] * 4 + [near] * 5,
        out_specs=near,
        scratch_shapes=[
            pltpu.VMEM((LEAD + ROWS, COLS), BF16),
            pltpu.VMEM((2 * (LEAD + ROWS), STATE), BF16),
            pltpu.VMEM((ROWS, COLS), BF16),
            pltpu.VMEM((HEADS, ROWS), F32),
            pltpu.VMEM((LEAD + ROWS, WIDE), F32),
            pltpu.VMEM((2 * (LEAD + ROWS), STATE), F32),
            pltpu.VMEM((PARTS, ROWS, WIDE), BF16),
            pltpu.VMEM((ROWS, STATE), BF16),
            pltpu.VMEM((BLOCKS, STATE, BLOCK), BF16),
            pltpu.VMEM((ROWS, 2 * STATE), BF16),
            pltpu.VMEM((BLOCKS * HEADS, BLOCK), F32),
            pltpu.VMEM((BLOCKS * HEADS, BLOCK), F32),
            pltpu.VMEM((BLOCKS, BLOCK, 2 * HEADS), BF16),
            pltpu.VMEM((BLOCKS, BLOCK, 5 * HEADS), BF16),
            pltpu.VMEM((2 * HEADS, COLS), BF16),
            pltpu.VMEM((PARTS, 32, WIDE), F32),
            pltpu.VMEM((8, COLS), F32),
            pltpu.VMEM((PARTS, STATE, WIDE), F32),
            pltpu.VMEM((PARTS, BLOCKS, STATE, WIDE), F32),
            pltpu.VMEM((BLOCKS, BLOCK, BLOCK), F32),
            pltpu.VMEM((ROWS, WIDE), F32),
            pltpu.VMEM((ROWS, WIDE), F32),
            pltpu.VMEM((PARTS, ROWS, WIDE), BF16),
            pltpu.VMEM((8, PARTS, TARGET, WIDE), BF16),
            pltpu.VMEM((PARTS, STATE, WIDE), F32),
            pltpu.VMEM((PARTS, ZS, SLICE, WIDE), BF16),
            pltpu.VMEM((PARTS, ZS, SLICE, WIDE), F32),
            pltpu.VMEM((PARTS, STATE, WIDE), BF16),
            pltpu.VMEM((PARTS, XS, SLICE, WIDE), F32),
            pltpu.VMEM((PARTS, ZS, SLICE, WIDE), F32),
            pltpu.VMEM((PARTS, 2, STATE, WIDE), F32),
            pltpu.VMEM((8, 128), F32),
            pltpu.VMEM((ZS, 8, 128), F32),
            pltpu.VMEM((8, 128), F32),
            pltpu.VMEM((XS, 8, 128), F32),
            pltpu.VMEM((2 * ZS, COLS), F32),
            pltpu.VMEM((8, COLS), F32),
            pltpu.VMEM((4, PASS, 8, BLOCK), F32),
            pltpu.VMEM((8, PASS, 8, BLOCK), F32),
            pltpu.VMEM((PASS * BLOCK, 128), F32),
            pltpu.VMEM((8, TARGET, 128), F32),
            dma((5,)),
            dma((3,)), dma((3,)),
            dma((ZS,)), dma((ZS,)),
            dma((XS,)), dma((XS,)),
            dma((PARTS, ZS)), dma((PARTS, ZS)),
            dma((PARTS, XS)), dma((PARTS, XS)),
            dma((PARTS, ZS)), dma((PARTS, ZS)),
            dma((PARTS, 4, 2)), dma((PARTS, 8)), dma((PARTS,)),
            dma((4, 2)), dma((8,)),
        ],
        compiler_params=pltpu.CompilerParams(
            collective_id=0, has_side_effects=True, vmem_limit_bytes=60 * 2**20
        ),
    )(
        channels_in,
        state_maps.reshape(2 * ROWS, STATE),
        gate_in,
        step_raw.T,
        convolution_channel_taps,
        conv_maps,
        head_rates,
        skip_gain.reshape(1, HEADS),
        norm_gain.reshape(1, COLS),
    )


def solution(mesh):
    return jax.shard_map(
        per_device,
        mesh=mesh,
        in_specs=(
            P("ctx", "head"),
            P("ctx", None, "head"),
            P("ctx", "head"),
            P("ctx", "head"),
            P(None, "head"),
            P(None, None, "head"),
            P(None, "head"),
            P("head"),
            P("head"),
        ),
        out_specs=P(("ctx", "head"), None),
        check_vma=False,
    )
```

```python
import jax
import jax.numpy as jnp
from jax import lax
from jax.experimental import pallas as pl
from jax.experimental.pallas import tpu as pltpu
from jax.sharding import PartitionSpec as P

HEAD_DIM = 64
STATE = 128
TAPS = 4
EPSILON = 1e-05
HI = lax.Precision.HIGHEST
MESH = pl.DeviceIdType.MESH
F32 = jnp.float32
BF16 = jnp.bfloat16

ROWS = 1536
COLS = 1024
HEADS = 16
BLOCK = 128
BLOCKS = ROWS // BLOCK
PARTS = 8
WIDE = COLS // PARTS
ZS = 8
XS = 4
SLICE = STATE // ZS
LEAD = 16
TARGET = ROWS // 8
PER = WIDE // HEAD_DIM
PASS = 3
HELD = 1
UNROLL = 4


def iota(shape, dim):
    return lax.broadcasted_iota(jnp.int32, shape, dim)


def dot(a, b, precision=None):
    return jnp.dot(a, b, precision=precision, preferred_element_type=F32)


def silu(v):
    half = 0.5 * v
    return half + half * jnp.tanh(half)


def split_in_two(v):
    high = v.astype(BF16).astype(F32)
    return high, v - high


def kernel(
    ch_hbm, bc_hbm, gate_hbm, step_hbm, taps, map_taps, rates, skip, gain, out,
    ch, bc, gate, step, wide, wide_maps, xs, bs, bt, cs, cum_v, step_v, tails, columns, spread,
    rows_v, skip_v, first_v, entering, scores_v, y0, squares, staged, landed,
    zs, z1, prefix, xt, x1, back, base, dl, dl_in, tl, tl_in, za, xa, scale_v, scale_in, scale_w, scale_all,
    in_sem, halo_s, halo_r, dl_s, dl_r, tl_s, tl_r, z1_s, z1_r, x1_s, x1_r, z2_s, z2_r,
    y_s, y_r, own_sem, n_s, n_r,
):
    c = lax.axis_index("ctx")
    me = lax.axis_index("head")
    x, z = c // ZS, c % ZS
    y, core = me // 2, me % 2

    rest = pl.ds(WIDE, COLS - WIDE)
    loads = [
        pltpu.make_async_copy(step_hbm, step, in_sem.at[0]),
        pltpu.make_async_copy(bc_hbm, bc.at[pl.ds(2 * LEAD, 2 * ROWS)], in_sem.at[1]),
        pltpu.make_async_copy(ch_hbm.at[:, pl.ds(0, WIDE)], ch.at[pl.ds(LEAD, ROWS), pl.ds(0, WIDE)], in_sem.at[2]),
        pltpu.make_async_copy(ch_hbm.at[:, rest], ch.at[pl.ds(LEAD, ROWS), rest], in_sem.at[3]),
        pltpu.make_async_copy(gate_hbm, gate, in_sem.at[4]),
    ]
    for load in loads[:3]:
        load.start()

    def z_peer(d):
        return (x * ZS + (z + d) % ZS, me)

    def x_peer(d):
        return (((x + d) % XS) * ZS + z, me)

    after, before = ((c + 1) % (XS * ZS), me), ((c + XS * ZS - 1) % (XS * ZS), me)
    peers = [z_peer(d) for d in range(1, ZS)] + [x_peer(d) for d in range(1, XS)]
    peers += [(c, (me + d) % 8) for d in range(1, 8)] + [after, before]
    barrier = pltpu.get_barrier_semaphore()
    for peer in peers:
        pl.semaphore_signal(barrier, inc=1, device_id=peer, device_id_type=MESH)

    spread[...] = (iota((2 * HEADS, COLS), 0) % HEADS == iota((2 * HEADS, COLS), 1) // HEAD_DIM).astype(BF16)
    head_of = (iota((HEADS, COLS), 0) == iota((HEADS, COLS), 1) // HEAD_DIM).astype(F32)
    bias = jnp.broadcast_to(rates[0:1, :], (BLOCK, HEADS)).T
    rate = jnp.broadcast_to(jnp.exp(rates[1:2, :]), (BLOCK, HEADS)).T
    rate = jnp.concatenate([rate] * BLOCKS, 0)
    loads[0].wait()
    raw = jnp.concatenate([step[:, pl.ds(k * BLOCK, BLOCK)] + bias for k in range(BLOCKS)], 0)
    sizes = jnp.maximum(raw, 0.0) + jnp.log1p(jnp.exp(-jnp.abs(raw)))
    logs = -rate * sizes
    row, col = iota((BLOCK, BLOCK), 0), iota((BLOCK, BLOCK), 1)
    cum = dot(logs, (row <= col).astype(F32), HI)
    later = dot(logs, (row > col).astype(F32), HI)
    cum_v[...] = cum * 1.4426950408889634
    step_v[...] = sizes
    high, low = split_in_two(jnp.exp(later) * sizes)
    for k in range(BLOCKS):
        of = slice(k * HEADS, (k + 1) * HEADS)
        tails[k] = jnp.concatenate([high[of], low[of]], 0).T.astype(BF16)
    count = BLOCKS * HEADS
    own_head = (iota((count, HEADS), 0) % HEADS == iota((count, HEADS), 1)).astype(F32)
    own_block = (iota((16, count), 0) == iota((16, count), 1) // HEADS).astype(F32)
    totals = dot(own_block, cum[:, BLOCK - 1 : BLOCK] * own_head, HI)
    row, col = iota((16, 16), 0), iota((16, 16), 1)
    earlier = dot(((row > col) & (col > 0)).astype(F32), totals, HI)
    growth = jnp.exp(dot(jnp.concatenate([totals, earlier], 0), head_of, HI))
    for q in range(PARTS):
        rows_v[q] = growth[:, q * WIDE : (q + 1) * WIDE]
    skip_v[...] = dot(jnp.broadcast_to(skip[...], (8, HEADS)), head_of, HI)
    whole = jnp.broadcast_to(earlier[BLOCKS : BLOCKS + 1] + totals[0:1], (8, HEADS))
    dl[...] = dot(whole, (iota((HEADS, 128), 0) == iota((HEADS, 128), 1)).astype(F32), HI)

    pl.semaphore_wait(barrier, len(peers))
    ends = [
        (bc_hbm.at[pl.ds(2 * (ROWS - LEAD), 2 * LEAD)], bc.at[pl.ds(0, 2 * LEAD)]),
        *((ch_hbm.at[pl.ds(ROWS - LEAD, LEAD), at], ch.at[pl.ds(0, LEAD), at]) for at in (pl.ds(0, WIDE), rest)),
    ]
    halo = [
        pltpu.make_async_remote_copy(
            src_ref=source, dst_ref=held, send_sem=halo_s.at[i], recv_sem=halo_r.at[i],
            device_id=after, device_id_type=MESH,
        )
        for i, (source, held) in enumerate(ends)
    ]
    for copy in halo[:2]:
        copy.start()
    dl_in[z] = dl[...]
    dl_copies = [
        pltpu.make_async_remote_copy(
            src_ref=dl, dst_ref=dl_in.at[z], send_sem=dl_s.at[d], recv_sem=dl_r.at[d],
            device_id=z_peer(d), device_id_type=MESH,
        )
        for d in range(1, ZS)
    ]
    for copy in dl_copies:
        copy.start()
    halo[2].start()
    for load in loads[3:]:
        load.start()

    def conv(row, weight):
        total = weight(0) * row(LEAD - 3)
        for tap in range(1, TAPS):
            total += weight(tap) * row(LEAD - 3 + tap)
        return silu(total)

    def maps(k):
        rows = pl.ds(k * BLOCK, BLOCK)

        def each(i):
            return conv(
                lambda r: wide_maps[pl.ds(2 * (k * BLOCK + r) + i, BLOCK, stride=2), :],
                lambda tap: map_taps[tap, i : i + 1, :],
            )

        b = each(0)
        bs[rows, :] = b.astype(BF16)
        bt[k] = b.T.astype(BF16)
        c_map = each(1).astype(BF16)
        cs[rows, :STATE] = c_map
        cs[rows, STATE:] = c_map

    body, lead = pl.ds(LEAD, ROWS), pl.ds(0, LEAD)
    loads[1].wait()
    wide_maps[pl.ds(2 * LEAD, 2 * ROWS), :] = bc[pl.ds(2 * LEAD, 2 * ROWS), :].astype(F32)
    for k in range(1, BLOCKS):
        maps(k)

    def lanes_of(q):
        return pl.ds(pl.multiple_of(q * WIDE, WIDE), WIDE)

    def summary(q, k):
        part = lanes_of(q)
        weights = dot(tails[k], spread[:, part])
        value = conv(
            lambda r: wide[pl.ds(k * BLOCK + r, BLOCK), :], lambda tap: taps[tap : tap + 1, part]
        ).astype(BF16)
        xs[q, pl.ds(k * BLOCK, BLOCK), :] = value
        return dot(bt[k], (value.astype(F32) * weights).astype(BF16))

    def blocks_but_first(q):
        part = lanes_of(q)
        wide[body, :] = ch[body, part].astype(F32)
        state = jnp.zeros((STATE, WIDE), F32)
        entering[q, 0] = state
        for k in range(1, BLOCKS):
            entering[q, k] = state
            state = rows_v[q, k : k + 1, :] * state + summary(q, k)
        zs[q] = state

    mine = pl.ds(pl.multiple_of(z * SLICE, SLICE), SLICE)

    def z1_copies(q):
        copies = []
        for d in (4, 3, 5, 2, 6, 1, 7):
            there = pl.ds(pl.multiple_of(((z + d) % ZS) * SLICE, SLICE), SLICE)
            copies.append(
                pltpu.make_async_remote_copy(
                    src_ref=xt.at[q, there], dst_ref=z1.at[q, z], send_sem=z1_s.at[q, d],
                    recv_sem=z1_r.at[q, d], device_id=z_peer(d), device_id_type=MESH,
                )
            )
        return copies

    def x1_copies(q):
        return [
            pltpu.make_async_remote_copy(
                src_ref=x1.at[q, x], dst_ref=x1.at[q, x], send_sem=x1_s.at[q, d],
                recv_sem=x1_r.at[q, d], device_id=x_peer(d), device_id_type=MESH,
            )
            for d in (2, 1, 3)
        ]

    def z2_copies(q):
        return [
            pltpu.make_async_remote_copy(
                src_ref=back.at[q, (z + d) % ZS], dst_ref=base.at[q, 0, mine], send_sem=z2_s.at[q, d],
                recv_sem=z2_r.at[q, d], device_id=z_peer(d), device_id_type=MESH,
            )
            for d in (4, 3, 5, 2, 6, 1, 7)
        ]

    def first_block(q):
        wide[lead, :] = ch[lead, lanes_of(q)].astype(F32)
        leave(q, summary(q, 0))

    def leave(q, first):
        first_v[q] = first
        state = (zs[q] + rows_v[q, 16 + BLOCKS : 17 + BLOCKS, :] * first).astype(BF16)
        xt[q] = state
        z1[q, z] = xt[q, mine, :]
        for copy in z1_copies(q):
            copy.start()

    def shard_decays():
        for copy in dl_copies:
            copy.wait()
        each = jnp.concatenate([dl_in[i, 0:1, :] for i in range(ZS)], 0)
        ahead = dot((iota((ZS, ZS), 0) > iota((ZS, ZS), 1)).astype(F32), each, HI)
        both = jnp.concatenate([each, ahead], 0)
        za[...] = jnp.exp(dot(both[:, :HEADS], head_of, HI))
        tl[...] = jnp.broadcast_to(jnp.sum(each, 0, keepdims=True), (8, 128))
        tl_in[x] = tl[...]
        copies = [
            pltpu.make_async_remote_copy(
                src_ref=tl, dst_ref=tl_in.at[x], send_sem=tl_s.at[d], recv_sem=tl_r.at[d],
                device_id=x_peer(d), device_id_type=MESH,
            )
            for d in range(1, XS)
        ]
        for copy in copies:
            copy.start()
        return copies

    def ring_decays(copies):
        for copy in copies:
            copy.wait()
        each = jnp.concatenate([tl_in[i, 0:1, :] for i in range(XS)] * 2, 0)
        xa[...] = jnp.exp(dot(each[:, :HEADS], head_of, HI))

    def along_z(q):
        part = lanes_of(q)
        for copy in z1_copies(q):
            copy.wait()
        total = jnp.zeros((SLICE, WIDE), F32)
        for i in range(ZS):
            prefix[q, i] = total
            total = za[i : i + 1, part] * total + z1[q, i].astype(F32)
        x1[q, x] = total
        for copy in x1_copies(q):
            copy.start()

    def along_x(q):
        part = lanes_of(q)
        for copy in x1_copies(q):
            copy.wait()
        total = jnp.zeros((SLICE, WIDE), F32)
        for i in range(XS - 1):
            total = jnp.where(i < x, xa[i : i + 1, part] * total + x1[q, i], total)
        for i in range(ZS):
            back[q, i] = prefix[q, i] + za[ZS + i : ZS + i + 1, part] * total
        base[q, 0, mine, :] = back[q, z]
        for copy in z2_copies(q):
            copy.start()

    def blocks_alone():
        @pl.loop(0, BLOCKS // UNROLL)
        def _(j):
            for i in range(UNROLL):
                k = UNROLL * j + i
                rows = pl.ds(pl.multiple_of(k * BLOCK, BLOCK), BLOCK)
                scores = lax.dot_general(
                    cs[rows, :STATE], bs[rows, :], (((1,), (1,)), ((), ())), preferred_element_type=F32
                )
                scores_v[k] = jnp.where(iota((BLOCK, BLOCK), 0) >= iota((BLOCK, BLOCK), 1), scores, 0.0)
                sums = cum_v[pl.ds(pl.multiple_of(k * HEADS, HEADS), HEADS), :]
                high, low = split_in_two(sums)
                middle, low = split_in_two(low)
                parts = [high, middle, low, *split_in_two(jnp.exp2(sums))]
                columns[k] = jnp.concatenate(parts, 0).T.astype(BF16)

    def inside(q):
        part = lanes_of(q)
        left = iota((BLOCK, WIDE), 1) < HEAD_DIM
        pick = PER * q + iota((3 * HEADS, PER * BLOCK), 1) // BLOCK == iota((3 * HEADS, PER * BLOCK), 0) % HEADS
        pick = pick.astype(BF16)

        @pl.loop(0, BLOCKS // UNROLL)
        def _(j):
            for i in range(UNROLL):
                k = UNROLL * j + i
                rows = pl.ds(pl.multiple_of(k * BLOCK, BLOCK), BLOCK)
                down = dot(columns[k, :, : 3 * HEADS], pick)
                weights = []
                for h in range(PER):
                    at = pl.ds(k * HEADS + PER * q + h, 1)
                    gap = jnp.minimum(down[:, h * BLOCK : (h + 1) * BLOCK] - cum_v[at, :], 0.0)
                    weights.append((scores_v[k] * jnp.exp2(gap) * step_v[at, :]).astype(BF16))
                value = xs[q, rows, :]
                none = jnp.zeros_like(value)
                both = jnp.concatenate([jnp.where(left, value, none), jnp.where(left, none, value)], 0)
                y0[q % 2, rows, :] = dot(jnp.concatenate(weights, 1), both) + skip_v[0:1, part] * value.astype(F32)

    def send_of(q, t, to):
        delta = (4 * t * t + 2) % 5 * (1 - t // 3)
        there = (y + delta) % 4
        return pltpu.make_async_remote_copy(
            src_ref=staged.at[q, pl.ds(pl.multiple_of((2 * there + to) * TARGET, TARGET), TARGET)],
            dst_ref=landed.at[me, q], send_sem=y_s.at[q, t, to], recv_sem=y_r.at[q, me],
            device_id=(c, 2 * there + to), device_id_type=MESH,
        )

    def own_of(q):
        return pltpu.make_async_copy(
            staged.at[q, pl.ds(pl.multiple_of(me * TARGET, TARGET), TARGET)],
            landed.at[me, q], own_sem.at[q],
        )

    def scale_of(t, to):
        delta = (4 * t * t + 2) % 5 * (1 - t // 3)
        there = (y + delta) % 4
        return pltpu.make_async_remote_copy(
            src_ref=scale_v.at[there], dst_ref=scale_in.at[me], send_sem=n_s.at[t, to],
            recv_sem=n_r.at[me], device_id=(c, 2 * there + to), device_id_type=MESH,
        )

    def all_but_own(t, to, remote, own):
        @pl.when((t < 3) | (to != core))
        def _():
            remote()

        @pl.when((t == 3) & (to == core))
        def _():
            own()

    def ship(q, t, to):
        all_but_own(t, to, send_of(q, t, to).start, own_of(q).start)

    def finish(q, send):
        part = lanes_of(q)
        for copy in z2_copies(q):
            copy.wait()
        base[q, 1] = rows_v[q, 0:1, :] * base[q, 0] + first_v[q]

        @pl.loop(0, 4)
        def _(t):
            delta = (4 * t * t + 2) % 5 * (1 - t // 3)
            there = (y + delta) % 4
            for m in range(PASS):
                k = PASS * there + m
                rows = pl.ds(pl.multiple_of(k * BLOCK, BLOCK), BLOCK)
                state_in = entering[q, k] + rows_v[q, pl.ds(16 + k, 1), :] * base[q, jnp.minimum(k, 1)]
                high, low = split_in_two(state_in)
                from_state = dot(cs[rows, :], jnp.concatenate([high, low], 0).astype(BF16))
                decay = dot(columns[k, :, 3 * HEADS :], spread[:, part])
                value = (y0[q % 2, rows, :] + decay * from_state) * silu(gate[rows, part].astype(F32))
                square = jnp.where(q == 0, 0.0, squares[rows, :]) + value * value
                squares[rows, :] = square
                staged[q, rows, :] = (value * gain[0:1, part]).astype(BF16)
                if send and m > 0:
                    ship(q, t, m - 1)

    def scales():
        @pl.loop(0, 4)
        def _(t):
            delta = (4 * t * t + 2) % 5 * (1 - t // 3)
            there = (y + delta) % 4
            for m in range(PASS):
                rows = pl.ds(pl.multiple_of((PASS * there + m) * BLOCK, BLOCK), BLOCK)
                scale = lax.rsqrt(jnp.sum(squares[rows, :], 1, keepdims=True) / COLS + EPSILON)
                scale_v[there, m] = jnp.broadcast_to(scale, (BLOCK, 128)).T[0:8, :]
            for to in range(2):

                def own():
                    scale_in[me] = scale_v[there]

                all_but_own(t, to, scale_of(t, to).start, own)

    loads[2].wait()
    blocks_but_first(0)
    ahead = pl.ds(0, 2 * LEAD)
    wide_maps[ahead, :] = jnp.zeros((2 * LEAD, STATE), F32)
    wide[lead, :] = jnp.zeros((LEAD, WIDE), F32)
    maps(0)
    weights = dot(tails[0], spread[:, :WIDE])
    value = conv(lambda r: wide[pl.ds(r, BLOCK), :], lambda tap: taps[tap : tap + 1, :WIDE]).astype(BF16)
    xs[0, pl.ds(0, BLOCK), :] = value
    tail = jnp.where(iota((BLOCK, WIDE), 0) < TAPS - 1, 0.0, value.astype(F32) * weights)
    first_v[0] = dot(bt[0], tail.astype(BF16))
    for copy in halo[:2]:
        copy.wait()
    inner = jnp.where(c == 0, 0.0, 1.0)
    wide_maps[ahead, :] = bc[ahead, :].astype(F32) * inner
    wide[lead, :] = ch[lead, pl.ds(0, WIDE)].astype(F32) * inner
    b_head = conv(
        lambda r: wide_maps[pl.ds(2 * r, LEAD, stride=2), :], lambda tap: map_taps[tap, 0:1, :]
    ).astype(BF16)
    value = conv(lambda r: wide[pl.ds(r, LEAD), :], lambda tap: taps[tap : tap + 1, :WIDE]).astype(BF16)
    xs[0, lead, :] = value
    tail = jnp.where(iota((LEAD, WIDE), 0) < TAPS - 1, value.astype(F32) * weights[:LEAD], 0.0)
    leave(0, first_v[0] + lax.dot_general(
        b_head, tail.astype(BF16), (((0,), (0,)), ((), ())), preferred_element_type=F32
    ))
    maps(0)
    loads[3].wait()
    halo[2].wait()

    @pl.when(c == 0)
    def _():
        ch[lead, rest] = jnp.zeros((LEAD, COLS - WIDE), BF16)

    @pl.loop(1, 4)
    def _(q):
        blocks_but_first(q)
        first_block(q)

    rings = shard_decays()
    along_z(0)
    blocks_alone()

    @pl.loop(4, 6)
    def _(i):
        blocks_but_first(i)
        first_block(i)
        along_z(i - 3)

        @pl.when(i == 4)
        def _():
            inside(0)
            ring_decays(rings)
            along_x(0)

    loads[4].wait()

    exchanges = {
        6: ((along_x, 2), (along_z, 3), (along_z, 4)),
        7: ((along_x, 3), (along_x, 4), (along_z, 5)),
        9: ((along_z, 6),),
        10: ((along_z, 7),),
    }
    exchanges_later = {8: ((along_x, 5),), 10: ((along_x, 6),), 11: ((along_x, 7),)}

    def at_step(i, step, calls):
        @pl.when(i == step)
        def _():
            for what, q in calls:
                what(q)

    along_x(1)

    @pl.loop(6, 13 - HELD)
    def _(i):
        finish(i - 6, True)
        for step, calls in exchanges.items():
            at_step(i, step, calls)
        inside(i - 5)

        @pl.when((i == 7) | (i == 8))
        def _():
            blocks_but_first(i - 1)
            first_block(i - 1)

        for step, calls in exchanges_later.items():
            at_step(i, step, calls)

    @pl.loop(13 - HELD, 14 - HELD)
    def _(i):
        finish(i - 6, True)

        @pl.when(i < PARTS + 5)
        def _():
            inside(i - 5)

    @pl.loop(14 - HELD, 14)
    def _(i):
        finish(i - 6, False)

        @pl.when(i < PARTS + 5)
        def _():
            inside(i - 5)

    scales()

    @pl.loop(PARTS - HELD, PARTS)
    def _(q):
        @pl.loop(0, 4)
        def _(t):
            for to in range(2):
                ship(q, t, to)

    def spread_scale(source):
        for m in range(PASS):
            scale_w[pl.ds(m * BLOCK, BLOCK), :] = jnp.broadcast_to(scale_in[source, m, 0:1, :], (128, BLOCK)).T
        scale_all[source] = scale_w[pl.ds(pl.multiple_of(core * TARGET, TARGET), TARGET), :]

    def place(source, q):
        lanes = pl.ds(pl.multiple_of(source * COLS + q * WIDE, WIDE), WIDE)
        out[:, lanes] = (landed[source, q].astype(F32) * scale_all[source]).astype(BF16)

    spread_scale(me)

    @pl.loop(0, PARTS)
    def _(q):
        own_of(q).wait()
        place(me, q)

    @pl.loop(1, 8)
    def _(d):
        source = (me + d) % 8
        pltpu.make_async_remote_copy(
            src_ref=scale_v.at[0], dst_ref=scale_in.at[source], send_sem=n_s.at[0, 0],
            recv_sem=n_r.at[source], device_id=(c, source), device_id_type=MESH,
        ).wait_recv()
        spread_scale(source)

    @pl.loop(0, PARTS)
    def _(q):
        @pl.loop(1, 8)
        def _(d):
            source = (me + d) % 8
            pltpu.make_async_remote_copy(
                src_ref=staged.at[q, pl.ds(0, TARGET)], dst_ref=landed.at[source, q],
                send_sem=y_s.at[q, 0, 0], recv_sem=y_r.at[q, source],
                device_id=(c, source), device_id_type=MESH,
            ).wait_recv()
            place(source, q)

    @pl.loop(0, 4)
    def _(t):
        for to in range(2):

            def remote():
                for q in range(PARTS):
                    send_of(q, t, to).wait_send()
                scale_of(t, to).wait_send()

            all_but_own(t, to, remote, lambda: None)


def per_device(
    channels_in,
    state_maps,
    gate_in,
    step_raw,
    convolution_channel_taps,
    conv_maps,
    head_rates,
    skip_gain,
    norm_gain,
):
    anywhere = pl.BlockSpec(memory_space=pl.ANY)
    near = pl.BlockSpec(memory_space=pltpu.VMEM)
    dma = pltpu.SemaphoreType.DMA
    return pl.pallas_call(
        kernel,
        out_shape=pltpu.VMEM((TARGET, COLS * 8), BF16),
        in_specs=[anywhere] * 4 + [near] * 5,
        out_specs=near,
        scratch_shapes=[
            pltpu.VMEM((LEAD + ROWS, COLS), BF16),
            pltpu.VMEM((2 * (LEAD + ROWS), STATE), BF16),
            pltpu.VMEM((ROWS, COLS), BF16),
            pltpu.VMEM((HEADS, ROWS), F32),
            pltpu.VMEM((LEAD + ROWS, WIDE), F32),
            pltpu.VMEM((2 * (LEAD + ROWS), STATE), F32),
            pltpu.VMEM((PARTS, ROWS, WIDE), BF16),
            pltpu.VMEM((ROWS, STATE), BF16),
            pltpu.VMEM((BLOCKS, STATE, BLOCK), BF16),
            pltpu.VMEM((ROWS, 2 * STATE), BF16),
            pltpu.VMEM((BLOCKS * HEADS, BLOCK), F32),
            pltpu.VMEM((BLOCKS * HEADS, BLOCK), F32),
            pltpu.VMEM((BLOCKS, BLOCK, 2 * HEADS), BF16),
            pltpu.VMEM((BLOCKS, BLOCK, 5 * HEADS), BF16),
            pltpu.VMEM((2 * HEADS, COLS), BF16),
            pltpu.VMEM((PARTS, 32, WIDE), F32),
            pltpu.VMEM((8, COLS), F32),
            pltpu.VMEM((PARTS, STATE, WIDE), F32),
            pltpu.VMEM((PARTS, BLOCKS, STATE, WIDE), F32),
            pltpu.VMEM((BLOCKS, BLOCK, BLOCK), F32),
            pltpu.VMEM((2, ROWS, WIDE), F32),
            pltpu.VMEM((ROWS, WIDE), F32),
            pltpu.VMEM((PARTS, ROWS, WIDE), BF16),
            pltpu.VMEM((8, PARTS, TARGET, WIDE), BF16),
            pltpu.VMEM((PARTS, STATE, WIDE), F32),
            pltpu.VMEM((PARTS, ZS, SLICE, WIDE), BF16),
            pltpu.VMEM((PARTS, ZS, SLICE, WIDE), F32),
            pltpu.VMEM((PARTS, STATE, WIDE), BF16),
            pltpu.VMEM((PARTS, XS, SLICE, WIDE), F32),
            pltpu.VMEM((PARTS, ZS, SLICE, WIDE), F32),
            pltpu.VMEM((PARTS, 2, STATE, WIDE), F32),
            pltpu.VMEM((8, 128), F32),
            pltpu.VMEM((ZS, 8, 128), F32),
            pltpu.VMEM((8, 128), F32),
            pltpu.VMEM((XS, 8, 128), F32),
            pltpu.VMEM((2 * ZS, COLS), F32),
            pltpu.VMEM((8, COLS), F32),
            pltpu.VMEM((4, PASS, 8, BLOCK), F32),
            pltpu.VMEM((8, PASS, 8, BLOCK), F32),
            pltpu.VMEM((PASS * BLOCK, 128), F32),
            pltpu.VMEM((8, TARGET, 128), F32),
            dma((5,)),
            dma((3,)), dma((3,)),
            dma((ZS,)), dma((ZS,)),
            dma((XS,)), dma((XS,)),
            dma((PARTS, ZS)), dma((PARTS, ZS)),
            dma((PARTS, XS)), dma((PARTS, XS)),
            dma((PARTS, ZS)), dma((PARTS, ZS)),
            dma((PARTS, 4, 2)), dma((PARTS, 8)), dma((PARTS,)),
            dma((4, 2)), dma((8,)),
        ],
        compiler_params=pltpu.CompilerParams(
            collective_id=0, has_side_effects=True, vmem_limit_bytes=60 * 2**20
        ),
    )(
        channels_in,
        state_maps.reshape(2 * ROWS, STATE),
        gate_in,
        step_raw.T,
        convolution_channel_taps,
        conv_maps,
        head_rates,
        skip_gain.reshape(1, HEADS),
        norm_gain.reshape(1, COLS),
    )


def solution(mesh):
    return jax.shard_map(
        per_device,
        mesh=mesh,
        in_specs=(
            P("ctx", "head"),
            P("ctx", None, "head"),
            P("ctx", "head"),
            P("ctx", "head"),
            P(None, "head"),
            P(None, None, "head"),
            P(None, "head"),
            P("head"),
            P("head"),
        ),
        out_specs=P(("ctx", "head"), None),
        check_vma=False,
    )
```

```python
import jax
import jax.numpy as jnp
from jax import lax
from jax.experimental import pallas as pl
from jax.experimental.pallas import tpu as pltpu
from jax.sharding import PartitionSpec as P

HEAD_DIM = 64
STATE = 128
TAPS = 4
EPSILON = 1e-05
HI = lax.Precision.HIGHEST
MESH = pl.DeviceIdType.MESH
F32 = jnp.float32
BF16 = jnp.bfloat16

ROWS = 1536
COLS = 1024
HEADS = 16
BLOCK = 128
BLOCKS = ROWS // BLOCK
PARTS = 8
WIDE = COLS // PARTS
ZS = 8
XS = 4
SLICE = STATE // ZS
LEAD = 16
TARGET = ROWS // 8
PER = WIDE // HEAD_DIM
PASS = 3
HELD = 1
UNROLL = 6


def iota(shape, dim):
    return lax.broadcasted_iota(jnp.int32, shape, dim)


def dot(a, b, precision=None):
    return jnp.dot(a, b, precision=precision, preferred_element_type=F32)


def silu(v):
    half = 0.5 * v
    return half + half * jnp.tanh(half)


def split_in_two(v):
    high = v.astype(BF16).astype(F32)
    return high, v - high


def kernel(
    ch_hbm, bc_hbm, gate_hbm, step_hbm, taps, map_taps, rates, skip, gain, out,
    ch, bc, gate, step, wide, wide_maps, xs, bs, bt, cs, cum_v, step_v, tails, columns, spread,
    rows_v, skip_v, first_v, entering, scores_v, y0, squares, staged, landed,
    zs, z1, prefix, xt, x1, back, base, dl, dl_in, tl, tl_in, za, xa, scale_v, scale_in, scale_w, scale_all,
    in_sem, halo_s, halo_r, dl_s, dl_r, tl_s, tl_r, z1_s, z1_r, x1_s, x1_r, z2_s, z2_r,
    y_s, y_r, own_sem, n_s, n_r,
):
    c = lax.axis_index("ctx")
    me = lax.axis_index("head")
    x, z = c // ZS, c % ZS
    y, core = me // 2, me % 2

    rest = pl.ds(WIDE, COLS - WIDE)
    loads = [
        pltpu.make_async_copy(step_hbm, step, in_sem.at[0]),
        pltpu.make_async_copy(bc_hbm, bc.at[pl.ds(2 * LEAD, 2 * ROWS)], in_sem.at[1]),
        pltpu.make_async_copy(ch_hbm.at[:, pl.ds(0, WIDE)], ch.at[pl.ds(LEAD, ROWS), pl.ds(0, WIDE)], in_sem.at[2]),
        pltpu.make_async_copy(ch_hbm.at[:, rest], ch.at[pl.ds(LEAD, ROWS), rest], in_sem.at[3]),
        pltpu.make_async_copy(gate_hbm, gate, in_sem.at[4]),
    ]
    for load in loads[:3]:
        load.start()

    def z_peer(d):
        return (x * ZS + (z + d) % ZS, me)

    def x_peer(d):
        return (((x + d) % XS) * ZS + z, me)

    after, before = ((c + 1) % (XS * ZS), me), ((c + XS * ZS - 1) % (XS * ZS), me)
    peers = [z_peer(d) for d in range(1, ZS)] + [x_peer(d) for d in range(1, XS)]
    peers += [(c, (me + d) % 8) for d in range(1, 8)] + [after, before]
    barrier = pltpu.get_barrier_semaphore()
    for peer in peers:
        pl.semaphore_signal(barrier, inc=1, device_id=peer, device_id_type=MESH)

    spread[...] = (iota((2 * HEADS, COLS), 0) % HEADS == iota((2 * HEADS, COLS), 1) // HEAD_DIM).astype(BF16)
    head_of = (iota((HEADS, COLS), 0) == iota((HEADS, COLS), 1) // HEAD_DIM).astype(F32)
    bias = jnp.broadcast_to(rates[0:1, :], (BLOCK, HEADS)).T
    rate = jnp.broadcast_to(jnp.exp(rates[1:2, :]), (BLOCK, HEADS)).T
    rate = jnp.concatenate([rate] * BLOCKS, 0)
    loads[0].wait()
    raw = jnp.concatenate([step[:, pl.ds(k * BLOCK, BLOCK)] + bias for k in range(BLOCKS)], 0)
    sizes = jnp.maximum(raw, 0.0) + jnp.log1p(jnp.exp(-jnp.abs(raw)))
    logs = -rate * sizes
    row, col = iota((BLOCK, BLOCK), 0), iota((BLOCK, BLOCK), 1)
    cum = dot(logs, (row <= col).astype(F32), HI)
    later = dot(logs, (row > col).astype(F32), HI)
    cum_v[...] = cum * 1.4426950408889634
    step_v[...] = sizes
    high, low = split_in_two(jnp.exp(later) * sizes)
    for k in range(BLOCKS):
        of = slice(k * HEADS, (k + 1) * HEADS)
        tails[k] = jnp.concatenate([high[of], low[of]], 0).T.astype(BF16)
    count = BLOCKS * HEADS
    own_head = (iota((count, HEADS), 0) % HEADS == iota((count, HEADS), 1)).astype(F32)
    own_block = (iota((16, count), 0) == iota((16, count), 1) // HEADS).astype(F32)
    totals = dot(own_block, cum[:, BLOCK - 1 : BLOCK] * own_head, HI)
    row, col = iota((16, 16), 0), iota((16, 16), 1)
    earlier = dot(((row > col) & (col > 0)).astype(F32), totals, HI)
    growth = jnp.exp(dot(jnp.concatenate([totals, earlier], 0), head_of, HI))
    for q in range(PARTS):
        rows_v[q] = growth[:, q * WIDE : (q + 1) * WIDE]
    skip_v[...] = dot(jnp.broadcast_to(skip[...], (8, HEADS)), head_of, HI)
    whole = jnp.broadcast_to(earlier[BLOCKS : BLOCKS + 1] + totals[0:1], (8, HEADS))
    dl[...] = dot(whole, (iota((HEADS, 128), 0) == iota((HEADS, 128), 1)).astype(F32), HI)

    pl.semaphore_wait(barrier, len(peers))
    ends = [
        (bc_hbm.at[pl.ds(2 * (ROWS - LEAD), 2 * LEAD)], bc.at[pl.ds(0, 2 * LEAD)]),
        *((ch_hbm.at[pl.ds(ROWS - LEAD, LEAD), at], ch.at[pl.ds(0, LEAD), at]) for at in (pl.ds(0, WIDE), rest)),
    ]
    halo = [
        pltpu.make_async_remote_copy(
            src_ref=source, dst_ref=held, send_sem=halo_s.at[i], recv_sem=halo_r.at[i],
            device_id=after, device_id_type=MESH,
        )
        for i, (source, held) in enumerate(ends)
    ]
    for copy in halo[:2]:
        copy.start()
    dl_in[z] = dl[...]
    dl_copies = [
        pltpu.make_async_remote_copy(
            src_ref=dl, dst_ref=dl_in.at[z], send_sem=dl_s.at[d], recv_sem=dl_r.at[d],
            device_id=z_peer(d), device_id_type=MESH,
        )
        for d in range(1, ZS)
    ]
    for copy in dl_copies:
        copy.start()
    halo[2].start()
    for load in loads[3:]:
        load.start()

    def conv(row, weight):
        total = weight(0) * row(LEAD - 3)
        for tap in range(1, TAPS):
            total += weight(tap) * row(LEAD - 3 + tap)
        return silu(total)

    def maps(k):
        rows = pl.ds(k * BLOCK, BLOCK)

        def each(i):
            return conv(
                lambda r: wide_maps[pl.ds(2 * (k * BLOCK + r) + i, BLOCK, stride=2), :],
                lambda tap: map_taps[tap, i : i + 1, :],
            )

        b = each(0)
        bs[rows, :] = b.astype(BF16)
        bt[k] = b.T.astype(BF16)
        c_map = each(1).astype(BF16)
        cs[rows, :STATE] = c_map
        cs[rows, STATE:] = c_map

    body, lead = pl.ds(LEAD, ROWS), pl.ds(0, LEAD)
    loads[1].wait()
    wide_maps[pl.ds(2 * LEAD, 2 * ROWS), :] = bc[pl.ds(2 * LEAD, 2 * ROWS), :].astype(F32)
    for k in range(1, BLOCKS):
        maps(k)

    def lanes_of(q):
        return pl.ds(pl.multiple_of(q * WIDE, WIDE), WIDE)

    def summary(q, k):
        part = lanes_of(q)
        weights = dot(tails[k], spread[:, part])
        value = conv(
            lambda r: wide[pl.ds(k * BLOCK + r, BLOCK), :], lambda tap: taps[tap : tap + 1, part]
        ).astype(BF16)
        xs[q, pl.ds(k * BLOCK, BLOCK), :] = value
        return dot(bt[k], (value.astype(F32) * weights).astype(BF16))

    def blocks_but_first(q):
        part = lanes_of(q)
        wide[body, :] = ch[body, part].astype(F32)
        state = jnp.zeros((STATE, WIDE), F32)
        entering[q, 0] = state
        for k in range(1, BLOCKS):
            entering[q, k] = state
            state = rows_v[q, k : k + 1, :] * state + summary(q, k)
        zs[q] = state

    mine = pl.ds(pl.multiple_of(z * SLICE, SLICE), SLICE)

    def z1_copies(q):
        copies = []
        for d in (4, 3, 5, 2, 6, 1, 7):
            there = pl.ds(pl.multiple_of(((z + d) % ZS) * SLICE, SLICE), SLICE)
            copies.append(
                pltpu.make_async_remote_copy(
                    src_ref=xt.at[q, there], dst_ref=z1.at[q, z], send_sem=z1_s.at[q, d],
                    recv_sem=z1_r.at[q, d], device_id=z_peer(d), device_id_type=MESH,
                )
            )
        return copies

    def x1_copies(q):
        return [
            pltpu.make_async_remote_copy(
                src_ref=x1.at[q, x], dst_ref=x1.at[q, x], send_sem=x1_s.at[q, d],
                recv_sem=x1_r.at[q, d], device_id=x_peer(d), device_id_type=MESH,
            )
            for d in (2, 1, 3)
        ]

    def z2_copies(q):
        return [
            pltpu.make_async_remote_copy(
                src_ref=back.at[q, (z + d) % ZS], dst_ref=base.at[q, 0, mine], send_sem=z2_s.at[q, d],
                recv_sem=z2_r.at[q, d], device_id=z_peer(d), device_id_type=MESH,
            )
            for d in (4, 3, 5, 2, 6, 1, 7)
        ]

    def first_block(q):
        wide[lead, :] = ch[lead, lanes_of(q)].astype(F32)
        leave(q, summary(q, 0))

    def leave(q, first):
        first_v[q] = first
        state = (zs[q] + rows_v[q, 16 + BLOCKS : 17 + BLOCKS, :] * first).astype(BF16)
        xt[q] = state
        z1[q, z] = xt[q, mine, :]
        for copy in z1_copies(q):
            copy.start()

    def shard_decays():
        for copy in dl_copies:
            copy.wait()
        each = jnp.concatenate([dl_in[i, 0:1, :] for i in range(ZS)], 0)
        ahead = dot((iota((ZS, ZS), 0) > iota((ZS, ZS), 1)).astype(F32), each, HI)
        both = jnp.concatenate([each, ahead], 0)
        za[...] = jnp.exp(dot(both[:, :HEADS], head_of, HI))
        tl[...] = jnp.broadcast_to(jnp.sum(each, 0, keepdims=True), (8, 128))
        tl_in[x] = tl[...]
        copies = [
            pltpu.make_async_remote_copy(
                src_ref=tl, dst_ref=tl_in.at[x], send_sem=tl_s.at[d], recv_sem=tl_r.at[d],
                device_id=x_peer(d), device_id_type=MESH,
            )
            for d in range(1, XS)
        ]
        for copy in copies:
            copy.start()
        return copies

    def ring_decays(copies):
        for copy in copies:
            copy.wait()
        each = jnp.concatenate([tl_in[i, 0:1, :] for i in range(XS)] * 2, 0)
        xa[...] = jnp.exp(dot(each[:, :HEADS], head_of, HI))

    def along_z(q):
        part = lanes_of(q)
        for copy in z1_copies(q):
            copy.wait()
        total = jnp.zeros((SLICE, WIDE), F32)
        for i in range(ZS):
            prefix[q, i] = total
            total = za[i : i + 1, part] * total + z1[q, i].astype(F32)
        x1[q, x] = total
        for copy in x1_copies(q):
            copy.start()

    def along_x(q):
        part = lanes_of(q)
        for copy in x1_copies(q):
            copy.wait()
        total = jnp.zeros((SLICE, WIDE), F32)
        for i in range(XS - 1):
            total = jnp.where(i < x, xa[i : i + 1, part] * total + x1[q, i], total)
        for i in range(ZS):
            back[q, i] = prefix[q, i] + za[ZS + i : ZS + i + 1, part] * total
        base[q, 0, mine, :] = back[q, z]
        for copy in z2_copies(q):
            copy.start()

    def blocks_alone():
        @pl.loop(0, BLOCKS // UNROLL)
        def _(j):
            for i in range(UNROLL):
                k = UNROLL * j + i
                rows = pl.ds(pl.multiple_of(k * BLOCK, BLOCK), BLOCK)
                scores = lax.dot_general(
                    cs[rows, :STATE], bs[rows, :], (((1,), (1,)), ((), ())), preferred_element_type=F32
                )
                scores_v[k] = jnp.where(iota((BLOCK, BLOCK), 0) >= iota((BLOCK, BLOCK), 1), scores, 0.0)
                sums = cum_v[pl.ds(pl.multiple_of(k * HEADS, HEADS), HEADS), :]
                high, low = split_in_two(sums)
                middle, low = split_in_two(low)
                parts = [high, middle, low, *split_in_two(jnp.exp2(sums))]
                columns[k] = jnp.concatenate(parts, 0).T.astype(BF16)

    def inside(q):
        part = lanes_of(q)
        left = iota((BLOCK, WIDE), 1) < HEAD_DIM
        pick = PER * q + iota((3 * HEADS, PER * BLOCK), 1) // BLOCK == iota((3 * HEADS, PER * BLOCK), 0) % HEADS
        pick = pick.astype(BF16)

        @pl.loop(0, BLOCKS // UNROLL)
        def _(j):
            for i in range(UNROLL):
                k = UNROLL * j + i
                rows = pl.ds(pl.multiple_of(k * BLOCK, BLOCK), BLOCK)
                down = dot(columns[k, :, : 3 * HEADS], pick)
                weights = []
                for h in range(PER):
                    at = pl.ds(k * HEADS + PER * q + h, 1)
                    gap = jnp.minimum(down[:, h * BLOCK : (h + 1) * BLOCK] - cum_v[at, :], 0.0)
                    weights.append((scores_v[k] * jnp.exp2(gap) * step_v[at, :]).astype(BF16))
                value = xs[q, rows, :]
                none = jnp.zeros_like(value)
                both = jnp.concatenate([jnp.where(left, value, none), jnp.where(left, none, value)], 0)
                y0[q % 2, rows, :] = dot(jnp.concatenate(weights, 1), both) + skip_v[0:1, part] * value.astype(F32)

    def send_of(q, t, to):
        delta = (4 * t * t + 2) % 5 * (1 - t // 3)
        there = (y + delta) % 4
        return pltpu.make_async_remote_copy(
            src_ref=staged.at[q, pl.ds(pl.multiple_of((2 * there + to) * TARGET, TARGET), TARGET)],
            dst_ref=landed.at[me, q], send_sem=y_s.at[q, t, to], recv_sem=y_r.at[q, me],
            device_id=(c, 2 * there + to), device_id_type=MESH,
        )

    def own_of(q):
        return pltpu.make_async_copy(
            staged.at[q, pl.ds(pl.multiple_of(me * TARGET, TARGET), TARGET)],
            landed.at[me, q], own_sem.at[q],
        )

    def scale_of(t, to):
        delta = (4 * t * t + 2) % 5 * (1 - t // 3)
        there = (y + delta) % 4
        return pltpu.make_async_remote_copy(
            src_ref=scale_v.at[there], dst_ref=scale_in.at[me], send_sem=n_s.at[t, to],
            recv_sem=n_r.at[me], device_id=(c, 2 * there + to), device_id_type=MESH,
        )

    def all_but_own(t, to, remote, own):
        @pl.when((t < 3) | (to != core))
        def _():
            remote()

        @pl.when((t == 3) & (to == core))
        def _():
            own()

    def ship(q, t, to):
        all_but_own(t, to, send_of(q, t, to).start, own_of(q).start)

    def finish(q, send):
        part = lanes_of(q)
        for copy in z2_copies(q):
            copy.wait()
        base[q, 1] = rows_v[q, 0:1, :] * base[q, 0] + first_v[q]

        @pl.loop(0, 4)
        def _(t):
            delta = (4 * t * t + 2) % 5 * (1 - t // 3)
            there = (y + delta) % 4
            for m in range(PASS):
                k = PASS * there + m
                rows = pl.ds(pl.multiple_of(k * BLOCK, BLOCK), BLOCK)
                state_in = entering[q, k] + rows_v[q, pl.ds(16 + k, 1), :] * base[q, jnp.minimum(k, 1)]
                high, low = split_in_two(state_in)
                from_state = dot(cs[rows, :], jnp.concatenate([high, low], 0).astype(BF16))
                decay = dot(columns[k, :, 3 * HEADS :], spread[:, part])
                value = (y0[q % 2, rows, :] + decay * from_state) * silu(gate[rows, part].astype(F32))
                square = jnp.where(q == 0, 0.0, squares[rows, :]) + value * value
                squares[rows, :] = square
                staged[q, rows, :] = (value * gain[0:1, part]).astype(BF16)
                if send and m > 0:
                    ship(q, t, m - 1)

    def scales():
        @pl.loop(0, 4)
        def _(t):
            delta = (4 * t * t + 2) % 5 * (1 - t // 3)
            there = (y + delta) % 4
            for m in range(PASS):
                rows = pl.ds(pl.multiple_of((PASS * there + m) * BLOCK, BLOCK), BLOCK)
                scale = lax.rsqrt(jnp.sum(squares[rows, :], 1, keepdims=True) / COLS + EPSILON)
                scale_v[there, m] = jnp.broadcast_to(scale, (BLOCK, 128)).T[0:8, :]
            for to in range(2):

                def own():
                    scale_in[me] = scale_v[there]

                all_but_own(t, to, scale_of(t, to).start, own)

    loads[2].wait()
    blocks_but_first(0)
    ahead = pl.ds(0, 2 * LEAD)
    wide_maps[ahead, :] = jnp.zeros((2 * LEAD, STATE), F32)
    wide[lead, :] = jnp.zeros((LEAD, WIDE), F32)
    maps(0)
    weights = dot(tails[0], spread[:, :WIDE])
    value = conv(lambda r: wide[pl.ds(r, BLOCK), :], lambda tap: taps[tap : tap + 1, :WIDE]).astype(BF16)
    xs[0, pl.ds(0, BLOCK), :] = value
    tail = jnp.where(iota((BLOCK, WIDE), 0) < TAPS - 1, 0.0, value.astype(F32) * weights)
    first_v[0] = dot(bt[0], tail.astype(BF16))
    for copy in halo[:2]:
        copy.wait()
    inner = jnp.where(c == 0, 0.0, 1.0)
    wide_maps[ahead, :] = bc[ahead, :].astype(F32) * inner
    wide[lead, :] = ch[lead, pl.ds(0, WIDE)].astype(F32) * inner
    b_head = conv(
        lambda r: wide_maps[pl.ds(2 * r, LEAD, stride=2), :], lambda tap: map_taps[tap, 0:1, :]
    ).astype(BF16)
    value = conv(lambda r: wide[pl.ds(r, LEAD), :], lambda tap: taps[tap : tap + 1, :WIDE]).astype(BF16)
    xs[0, lead, :] = value
    tail = jnp.where(iota((LEAD, WIDE), 0) < TAPS - 1, value.astype(F32) * weights[:LEAD], 0.0)
    leave(0, first_v[0] + lax.dot_general(
        b_head, tail.astype(BF16), (((0,), (0,)), ((), ())), preferred_element_type=F32
    ))
    maps(0)
    loads[3].wait()
    halo[2].wait()

    @pl.when(c == 0)
    def _():
        ch[lead, rest] = jnp.zeros((LEAD, COLS - WIDE), BF16)

    @pl.loop(1, 4)
    def _(q):
        blocks_but_first(q)
        first_block(q)

    rings = shard_decays()
    along_z(0)
    blocks_alone()

    @pl.loop(4, 6)
    def _(i):
        blocks_but_first(i)
        first_block(i)

        @pl.when(i == 5)
        def _():
            along_x(1)

        along_z(i - 3)

        @pl.when(i == 4)
        def _():
            inside(0)
            ring_decays(rings)
            along_x(0)

    loads[4].wait()

    exchanges = {
        6: ((along_x, 2), (along_z, 3), (along_z, 4)),
        7: ((along_x, 3), (along_x, 4), (along_z, 5)),
        9: ((along_z, 6),),
        10: ((along_z, 7),),
    }
    exchanges_later = {8: ((along_x, 5),), 10: ((along_x, 6),), 11: ((along_x, 7),)}

    def at_step(i, step, calls):
        @pl.when(i == step)
        def _():
            for what, q in calls:
                what(q)

    @pl.loop(6, 13 - HELD)
    def _(i):
        finish(i - 6, True)
        for step, calls in exchanges.items():
            at_step(i, step, calls)
        inside(i - 5)

        @pl.when((i == 7) | (i == 8))
        def _():
            blocks_but_first(i - 1)
            first_block(i - 1)

        for step, calls in exchanges_later.items():
            at_step(i, step, calls)

    @pl.loop(13 - HELD, 14 - HELD)
    def _(i):
        finish(i - 6, True)

        @pl.when(i < PARTS + 5)
        def _():
            inside(i - 5)

    @pl.loop(14 - HELD, 14)
    def _(i):
        finish(i - 6, False)

        @pl.when(i < PARTS + 5)
        def _():
            inside(i - 5)

    scales()

    @pl.loop(PARTS - HELD, PARTS)
    def _(q):
        @pl.loop(0, 4)
        def _(t):
            for to in range(2):
                ship(q, t, to)

    def spread_scale(source):
        for m in range(PASS):
            scale_w[pl.ds(m * BLOCK, BLOCK), :] = jnp.broadcast_to(scale_in[source, m, 0:1, :], (128, BLOCK)).T
        scale_all[source] = scale_w[pl.ds(pl.multiple_of(core * TARGET, TARGET), TARGET), :]

    def place(source, q):
        lanes = pl.ds(pl.multiple_of(source * COLS + q * WIDE, WIDE), WIDE)
        out[:, lanes] = (landed[source, q].astype(F32) * scale_all[source]).astype(BF16)

    spread_scale(me)

    @pl.loop(0, PARTS)
    def _(q):
        own_of(q).wait()
        place(me, q)

    @pl.loop(1, 8)
    def _(d):
        source = (me + d) % 8
        pltpu.make_async_remote_copy(
            src_ref=scale_v.at[0], dst_ref=scale_in.at[source], send_sem=n_s.at[0, 0],
            recv_sem=n_r.at[source], device_id=(c, source), device_id_type=MESH,
        ).wait_recv()
        spread_scale(source)

    @pl.loop(0, PARTS)
    def _(q):
        @pl.loop(1, 8)
        def _(d):
            source = (me + d) % 8
            pltpu.make_async_remote_copy(
                src_ref=staged.at[q, pl.ds(0, TARGET)], dst_ref=landed.at[source, q],
                send_sem=y_s.at[q, 0, 0], recv_sem=y_r.at[q, source],
                device_id=(c, source), device_id_type=MESH,
            ).wait_recv()
            place(source, q)

    @pl.loop(0, 4)
    def _(t):
        for to in range(2):

            def remote():
                for q in range(PARTS):
                    send_of(q, t, to).wait_send()
                scale_of(t, to).wait_send()

            all_but_own(t, to, remote, lambda: None)


def per_device(
    channels_in,
    state_maps,
    gate_in,
    step_raw,
    convolution_channel_taps,
    conv_maps,
    head_rates,
    skip_gain,
    norm_gain,
):
    anywhere = pl.BlockSpec(memory_space=pl.ANY)
    near = pl.BlockSpec(memory_space=pltpu.VMEM)
    dma = pltpu.SemaphoreType.DMA
    return pl.pallas_call(
        kernel,
        out_shape=pltpu.VMEM((TARGET, COLS * 8), BF16),
        in_specs=[anywhere] * 4 + [near] * 5,
        out_specs=near,
        scratch_shapes=[
            pltpu.VMEM((LEAD + ROWS, COLS), BF16),
            pltpu.VMEM((2 * (LEAD + ROWS), STATE), BF16),
            pltpu.VMEM((ROWS, COLS), BF16),
            pltpu.VMEM((HEADS, ROWS), F32),
            pltpu.VMEM((LEAD + ROWS, WIDE), F32),
            pltpu.VMEM((2 * (LEAD + ROWS), STATE), F32),
            pltpu.VMEM((PARTS, ROWS, WIDE), BF16),
            pltpu.VMEM((ROWS, STATE), BF16),
            pltpu.VMEM((BLOCKS, STATE, BLOCK), BF16),
            pltpu.VMEM((ROWS, 2 * STATE), BF16),
            pltpu.VMEM((BLOCKS * HEADS, BLOCK), F32),
            pltpu.VMEM((BLOCKS * HEADS, BLOCK), F32),
            pltpu.VMEM((BLOCKS, BLOCK, 2 * HEADS), BF16),
            pltpu.VMEM((BLOCKS, BLOCK, 5 * HEADS), BF16),
            pltpu.VMEM((2 * HEADS, COLS), BF16),
            pltpu.VMEM((PARTS, 32, WIDE), F32),
            pltpu.VMEM((8, COLS), F32),
            pltpu.VMEM((PARTS, STATE, WIDE), F32),
            pltpu.VMEM((PARTS, BLOCKS, STATE, WIDE), F32),
            pltpu.VMEM((BLOCKS, BLOCK, BLOCK), F32),
            pltpu.VMEM((2, ROWS, WIDE), F32),
            pltpu.VMEM((ROWS, WIDE), F32),
            pltpu.VMEM((PARTS, ROWS, WIDE), BF16),
            pltpu.VMEM((8, PARTS, TARGET, WIDE), BF16),
            pltpu.VMEM((PARTS, STATE, WIDE), F32),
            pltpu.VMEM((PARTS, ZS, SLICE, WIDE), BF16),
            pltpu.VMEM((PARTS, ZS, SLICE, WIDE), F32),
            pltpu.VMEM((PARTS, STATE, WIDE), BF16),
            pltpu.VMEM((PARTS, XS, SLICE, WIDE), F32),
            pltpu.VMEM((PARTS, ZS, SLICE, WIDE), F32),
            pltpu.VMEM((PARTS, 2, STATE, WIDE), F32),
            pltpu.VMEM((8, 128), F32),
            pltpu.VMEM((ZS, 8, 128), F32),
            pltpu.VMEM((8, 128), F32),
            pltpu.VMEM((XS, 8, 128), F32),
            pltpu.VMEM((2 * ZS, COLS), F32),
            pltpu.VMEM((8, COLS), F32),
            pltpu.VMEM((4, PASS, 8, BLOCK), F32),
            pltpu.VMEM((8, PASS, 8, BLOCK), F32),
            pltpu.VMEM((PASS * BLOCK, 128), F32),
            pltpu.VMEM((8, TARGET, 128), F32),
            dma((5,)),
            dma((3,)), dma((3,)),
            dma((ZS,)), dma((ZS,)),
            dma((XS,)), dma((XS,)),
            dma((PARTS, ZS)), dma((PARTS, ZS)),
            dma((PARTS, XS)), dma((PARTS, XS)),
            dma((PARTS, ZS)), dma((PARTS, ZS)),
            dma((PARTS, 4, 2)), dma((PARTS, 8)), dma((PARTS,)),
            dma((4, 2)), dma((8,)),
        ],
        compiler_params=pltpu.CompilerParams(
            collective_id=0, has_side_effects=True, vmem_limit_bytes=60 * 2**20
        ),
    )(
        channels_in,
        state_maps.reshape(2 * ROWS, STATE),
        gate_in,
        step_raw.T,
        convolution_channel_taps,
        conv_maps,
        head_rates,
        skip_gain.reshape(1, HEADS),
        norm_gain.reshape(1, COLS),
    )


def solution(mesh):
    return jax.shard_map(
        per_device,
        mesh=mesh,
        in_specs=(
            P("ctx", "head"),
            P("ctx", None, "head"),
            P("ctx", "head"),
            P("ctx", "head"),
            P(None, "head"),
            P(None, None, "head"),
            P(None, "head"),
            P("head"),
            P("head"),
        ),
        out_specs=P(("ctx", "head"), None),
        check_vma=False,
    )
```
